32 devices in a mesh: groups: 2 (over x), scan: 8 (over z, y), tile: 2 (over core).
Axes of the slice: x: 2, y: 2, z: 4, core: 2. Of those that a mesh axis runs over, the one named last changes fastest.
Arguments:
- object_field: float32 [2, 10240, 384], P(None, ('groups', 'scan', 'tile')), parts along dimension 1, may hold values from -6 to 6
- probe_modes: float32 [2, 32, 65536], P(None, 'groups', ('scan', 'tile')), parts along dimension 1, may hold values from -6 to 6
- weights: float32 [2, 256, 16], P(None, ('groups', 'scan', 'tile')), parts along dimension 1, may hold values from -1.2 to 1.2
- amplitude: bfloat16 [256, 256, 256], P(('groups', 'scan', 'tile')), parts along dimension 0, may hold values from 0 to 3
- slot_count: int32 [32], P(('groups', 'scan')), parts along dimension 0, may hold values from 1 to 8, 96 in all
- tile_owner: int32 [256], P(('groups', 'scan')), parts along dimension 0, may hold values from 0 to 1
- corner_row: int32 [256], P(('groups', 'scan')), parts along dimension 0, may hold values from 0 to 64
- corner_col: int32 [256], P(('groups', 'scan')), parts along dimension 0, may hold values from 0 to 128
Outputs:
- new_object: float32 [2, 10240, 384], P(None, ('groups', 'scan', 'tile')), parts along dimension 1
- new_modes: float32 [2, 32, 65536], P(None, 'groups', ('scan', 'tile')), parts along dimension 1
- new_weights: float32 [2, 256, 16], P(None, ('groups', 'scan', 'tile')), parts along dimension 1
The draws below stay inside these ranges and needn't reach their ends.
There are 2 independent parts, one for each index of `groups`. The reference program is written for one: setup_inputs(seed, part) draws one part's arguments, and reference() takes and returns one part's arrays. A program takes and returns all parts, laid end to end along the dimension named above; each array names one. Nothing has to cross between parts.
Inputs may be any that keep to these rules, and one draw needn't show every extreme that they name: slot_count[d] positions live on device d, in its slots 0 to slot_count[d] - 1; some device of every part holds 8. `tile_owner`: the tile, among the 2 tiles of the same scan index, whose rows hold the position's patch. `corner_row`: a patch lies wholly inside its tile's rows. `corner_col`: a patch lies wholly inside the object's columns.
All inputs are finite; a program needn't handle non-finite values.
Results may differ from the reference program's by a relative error of at most 0.0097.
Values may be sent and summed in bfloat16 or wider, within the bound.
No kernel may reach another device: no remote copies, remote signals or barrier semaphores. Data moves between devices by JAX's collectives and lax.ppermute only.
A program may use at most 128 MiB of HBM per device.

```python
import math
import jax
import jax.numpy as jnp
import numpy as np
from jax import lax

P_SIZE = 256
K = 16
CAP = 8
OT = 320
OW = 384
PIX = 65536
POS = 128
OBJ_ROWS = 5120
N_SCAN = 8
N_TILE = 2


def with_ends(array, stream_key, least, high):
    spot = [jax.random.randint(jax.random.fold_in(stream_key, axis), (), 0, length) for axis, length in enumerate(array.shape)]
    longest = array.shape.index(max(array.shape))
    neighbour = spot[:longest] + [(spot[longest] + 1) % array.shape[longest]] + spot[longest + 1:]
    return array.at[tuple(spot)].set(least).at[tuple(neighbour)].set(high)


def steps_of(rng, extent, shards, least, largest):
    level = 1.0
    for axis_at, shards_of in shards:
        steps = jax.random.uniform(jax.random.fold_in(jax.random.fold_in(rng, 6), axis_at), (shards_of,), jnp.float32, least / len(shards), largest / len(shards))
        level = level * jnp.repeat(jnp.exp(steps), extent[axis_at] // shards_of).reshape((-1,) + (1,) * (len(extent) - 1 - axis_at))
    return level


def length_profile(count, total, limit, slope):
    loads = [(1 << 20) // math.isqrt(grade ** slope) + 1 for grade in range(2, count + 1)]
    surplus, counts = total - limit - (count - 1), [1] * (count - 1)
    while surplus > 0:
        movable = [i for i in range(count - 1) if counts[i] < limit]
        pool, left = sum([loads[i] for i in movable]), surplus
        for i in movable:
            addition = min(limit - counts[i], max(1, left * loads[i] // pool), surplus)
            counts[i] = counts[i] + addition
            surplus = surplus - addition
    return np.array([limit] + counts)


def ragged_sizes(key, amount, total, most, skew):
    if amount == 2:
        one = jax.random.randint(key, (), max(1, total - most), min(most, total - 1) + 1)
        return jnp.stack([one, total - one])
    sizes = jnp.asarray(length_profile(amount, total, most, skew), jnp.int32)
    pairs = (amount - 1) // 2
    donor, receiver = sizes[1:1 + 2 * pairs:2], sizes[2:2 + 2 * pairs:2]
    slack = jnp.minimum(donor - 1, most - receiver)
    moved = jax.random.randint(jax.random.fold_in(key, 1), (pairs,), 0, 1 << 20) % (slack + 1)
    sizes = sizes.at[1:1 + 2 * pairs:2].set(donor - moved).at[2:2 + 2 * pairs:2].set(receiver + moved)
    return sizes[jax.random.permutation(jax.random.fold_in(key, 2), amount)]


def noise(key, dims, spread, reach, shards=(), kind=jnp.bfloat16):
    array = spread * jax.random.normal(key, dims, jnp.float32)
    if shards:
        array = array * steps_of(key, dims, shards, -0.22, 0.18)
    return jnp.clip(array, -reach, reach).astype(kind)


def setup_inputs(seed: int = 0, part: int = 0) -> dict:
    keys = jax.random.split(jax.random.key(seed), 9)
    part_keys = jax.random.split(jax.random.fold_in(keys[8], part), 9)
    return {
        "object_field": noise(part_keys[0], (2, OBJ_ROWS, OW), 1.0, 6.0, ((1, 16),), jnp.float32),
        "probe_modes": noise(part_keys[1], (2, K, PIX), 1.0, 6.0, ((2, 16),), jnp.float32),
        "weights": noise(part_keys[2], (2, POS, K), 0.2, 1.2, ((1, 16),), jnp.float32),
        "amplitude": jnp.clip(3.0 * jax.random.uniform(part_keys[3], (POS, P_SIZE, P_SIZE), jnp.float32) ** steps_of(part_keys[3], (POS, P_SIZE, P_SIZE), ((0, 16),), -0.2, 0.2), 0.0, 3.0).astype(jnp.bfloat16),
        "slot_count": ragged_sizes(part_keys[4], N_SCAN * N_TILE, (3 * N_SCAN * N_TILE * CAP) // 4, CAP, 2).astype(jnp.int32),
        "tile_owner": with_ends(jax.random.randint(part_keys[5], (POS,), 0, N_TILE), jax.random.fold_in(part_keys[5], 1), 0, N_TILE - 1).astype(jnp.int32),
        "corner_row": with_ends(jax.random.randint(part_keys[6], (POS,), 0, OT - P_SIZE + 1), jax.random.fold_in(part_keys[6], 1), 0, OT - P_SIZE).astype(jnp.int32),
        "corner_col": with_ends(jax.random.randint(part_keys[7], (POS,), 0, OW - P_SIZE + 1), jax.random.fold_in(part_keys[7], 1), 0, OW - P_SIZE).astype(jnp.int32),
    }


OBJ_STEP = 0.125
PROBE_STEP = 0.5
best_precision = lax.Precision.HIGHEST

def dft_tables(length):
    pixel_ids = jnp.arange(length, dtype=jnp.int32)
    phase_ids = pixel_ids[:, None] * pixel_ids[None, :] % length
    angles = phase_ids.astype(jnp.float32) * (2.0 * math.pi / length)
    norm_scale = 1.0 / math.sqrt(length)
    cos_tab = (jnp.cos(angles) * norm_scale).astype(jnp.bfloat16)
    sin_tab = (jnp.sin(angles) * norm_scale).astype(jnp.bfloat16)
    forward_rows = jnp.concatenate([jnp.concatenate([cos_tab, sin_tab], axis=1), jnp.concatenate([-sin_tab, cos_tab], axis=1)], axis=0)
    inverse_rows = jnp.concatenate([jnp.concatenate([cos_tab, -sin_tab], axis=1), jnp.concatenate([sin_tab, cos_tab], axis=1)], axis=0)
    return (cos_tab, sin_tab, forward_rows, inverse_rows)

def rows_pass(row_table, planes):
    count_pos = planes.shape[0]
    length = planes.shape[2]
    flat_planes = planes.reshape(count_pos, 2 * length, length).astype(jnp.float32)
    result = jnp.einsum('ij,njb->nib', row_table.astype(jnp.float32), flat_planes, precision=best_precision)
    return result.reshape(count_pos, 2, length, length)

def cols_pass(cos_tab, sin_tab, planes, direction):
    real_part = planes[:, 0].astype(jnp.float32)
    imag_part = planes[:, 1].astype(jnp.float32)
    cos_wide = cos_tab.astype(jnp.float32)
    sin_wide = sin_tab.astype(jnp.float32)
    out_real = jnp.einsum('nab,bk->nak', real_part, cos_wide, precision=best_precision) + direction * jnp.einsum('nab,bk->nak', imag_part, sin_wide, precision=best_precision)
    out_imag = jnp.einsum('nab,bk->nak', imag_part, cos_wide, precision=best_precision) - direction * jnp.einsum('nab,bk->nak', real_part, sin_wide, precision=best_precision)
    return jnp.stack([out_real, out_imag], axis=1)

def relax_positions(patch_b, probe_field, amp_block, live_mask, tables):
    cos_tab, sin_tab, forward_rows, inverse_rows = tables
    obj_real = patch_b[:, 0].astype(jnp.float32)
    obj_imag = patch_b[:, 1].astype(jnp.float32)
    probe_real = probe_field[:, 0]
    probe_imag = probe_field[:, 1]
    exit_wave = jnp.stack([probe_real * obj_real - probe_imag * obj_imag, probe_real * obj_imag + probe_imag * obj_real], axis=1).astype(jnp.bfloat16)
    sectioned = rows_pass(forward_rows, exit_wave).astype(jnp.bfloat16)
    far_field = cols_pass(cos_tab, sin_tab, sectioned, 1.0)
    power = far_field[:, 0] * far_field[:, 0] + far_field[:, 1] * far_field[:, 1]
    scale_map = amp_block.astype(jnp.float32) / jnp.sqrt(power + 1.0)
    revised = (far_field * scale_map[:, None]).astype(jnp.bfloat16)
    came_back = rows_pass(inverse_rows, revised).astype(jnp.bfloat16)
    near_field = cols_pass(cos_tab, sin_tab, came_back, -1.0)
    delta_field = near_field - exit_wave.astype(jnp.float32)
    delta_real = delta_field[:, 0]
    delta_imag = delta_field[:, 1]
    mask_wide = live_mask[:, None, None, None]
    grad_field = jnp.stack([probe_real * delta_real + probe_imag * delta_imag, probe_real * delta_imag - probe_imag * delta_real], axis=1) * mask_wide
    change = jnp.stack([obj_real * delta_real + obj_imag * delta_imag, obj_real * delta_imag - obj_imag * delta_real], axis=1)
    updated = (probe_field + PROBE_STEP * change) * mask_wide
    return (grad_field.astype(jnp.bfloat16), updated.astype(jnp.bfloat16))

def probe_mixing(weights_b):
    wt_real = weights_b[0]
    wt_imag = weights_b[1]
    slot_cap = wt_real.shape[0]
    mode_count = wt_real.shape[1]
    upper_rows = jnp.concatenate([wt_real, -wt_imag], axis=1)
    lower_rows = jnp.concatenate([wt_imag, wt_real], axis=1)
    return jnp.stack([upper_rows, lower_rows], axis=1).reshape(2 * slot_cap, 2 * mode_count)

def gather_mixing(weights_b):
    wt_real = weights_b[0]
    wt_imag = weights_b[1]
    slot_cap = wt_real.shape[0]
    mode_count = wt_real.shape[1]
    real_rows = jnp.stack([wt_real.T, wt_imag.T], axis=2)
    imag_rows = jnp.stack([-wt_imag.T, wt_real.T], axis=2)
    return jnp.stack([real_rows, imag_rows], axis=0).reshape(2 * mode_count, 2 * slot_cap)

def project_weights(updated_flat, basis_flat, slot_cap, mode_count, pixels):
    table_full = jnp.einsum('ip,jp->ij', updated_flat.astype(jnp.float32), basis_flat.astype(jnp.float32), precision=best_precision)
    table_full = table_full.reshape(slot_cap, 2, 2, mode_count)
    new_real = table_full[:, 0, 0] + table_full[:, 1, 1]
    new_imag = table_full[:, 1, 0] - table_full[:, 0, 1]
    return jnp.stack([new_real, new_imag], axis=0) / pixels

def mode_gram(mode_real, mode_imag):
    gram_real = jnp.dot(mode_real, mode_real.T, precision=best_precision) + jnp.dot(mode_imag, mode_imag.T, precision=best_precision)
    gram_imag = jnp.dot(mode_real, mode_imag.T, precision=best_precision) - jnp.dot(mode_imag, mode_real.T, precision=best_precision)
    return (gram_real, gram_imag)

def cholesky_factor(gram_real, gram_imag):
    width = gram_real.shape[0]
    col_ids = jnp.arange(width, dtype=jnp.int32)
    rows_real = []
    rows_imag = []
    for pivot in range(width):
        acc_real = gram_real[pivot]
        acc_imag = gram_imag[pivot]
        for earlier in range(pivot):
            lead_real = rows_real[earlier][pivot]
            lead_imag = rows_imag[earlier][pivot]
            acc_real = acc_real - (lead_real * rows_real[earlier] + lead_imag * rows_imag[earlier])
            acc_imag = acc_imag - (lead_real * rows_imag[earlier] - lead_imag * rows_real[earlier])
        pivot_root = jnp.sqrt(acc_real[pivot])
        rows_real.append(jnp.where(col_ids >= pivot, acc_real / pivot_root, 0.0))
        rows_imag.append(jnp.where(col_ids > pivot, acc_imag / pivot_root, 0.0))
    return (jnp.stack(rows_real), jnp.stack(rows_imag))

def solve_rows(mode_real, mode_imag, fac_real, fac_imag):
    width = mode_real.shape[0]
    solved_real = []
    solved_imag = []
    for pivot in range(width):
        acc_real = mode_real[pivot]
        acc_imag = mode_imag[pivot]
        for earlier in range(pivot):
            coef_real = fac_real[earlier, pivot]
            coef_imag = fac_imag[earlier, pivot]
            acc_real = acc_real - (coef_real * solved_real[earlier] - coef_imag * solved_imag[earlier])
            acc_imag = acc_imag - (coef_real * solved_imag[earlier] + coef_imag * solved_real[earlier])
        solved_real.append(acc_real / fac_real[pivot, pivot])
        solved_imag.append(acc_imag / fac_real[pivot, pivot])
    return jnp.stack([jnp.stack(solved_real), jnp.stack(solved_imag)])

def reference(object_field, probe_modes, weights, amplitude, slot_count, tile_owner, corner_row, corner_col):
    devices = N_SCAN * N_TILE
    pixels = P_SIZE * P_SIZE
    tables = dft_tables(P_SIZE)
    object_b = object_field.astype(jnp.bfloat16)
    basis_flat = probe_modes.astype(jnp.bfloat16).reshape(2 * K, pixels)
    weights_dev = weights.astype(jnp.bfloat16).reshape(2, devices, CAP, K).transpose(1, 0, 2, 3)
    amp_dev = amplitude.reshape(devices, CAP, P_SIZE, P_SIZE)
    owner_dev = tile_owner.reshape(devices, CAP)
    row_dev = corner_row.reshape(devices, CAP)
    col_dev = corner_col.reshape(devices, CAP)
    slot_ids = jnp.arange(CAP, dtype=jnp.int32)
    zero_index = jnp.zeros((), jnp.int32)

    def per_device(carry, inputs):
        grad_total, mode_total = carry
        dev_id, wt_block, amp_block, live_count, own_block, row_block, col_block = inputs
        live_mask = (slot_ids < live_count).astype(jnp.float32)
        abs_rows = ((dev_id // N_TILE * N_TILE + own_block) * OT + row_block).astype(jnp.int32)
        col_block = col_block.astype(jnp.int32)

        def cut_piece(row_at, col_at):
            return lax.dynamic_slice(object_b, (zero_index, row_at, col_at), (2, P_SIZE, P_SIZE))
        patch_b = jax.vmap(cut_piece)(abs_rows, col_block)
        probe_field = jnp.dot(probe_mixing(wt_block), basis_flat, preferred_element_type=jnp.float32).reshape(CAP, 2, P_SIZE, P_SIZE)
        grad_b, updated_b = relax_positions(patch_b, probe_field, amp_block, live_mask, tables)

        def add_own(position, grad_accum):
            grad_piece = lax.dynamic_index_in_dim(grad_b, position, 0, keepdims=False).astype(jnp.float32)
            row_at = lax.dynamic_index_in_dim(abs_rows, position, 0, keepdims=False)
            col_at = lax.dynamic_index_in_dim(col_block, position, 0, keepdims=False)
            old_block = lax.dynamic_slice(grad_accum, (zero_index, row_at, col_at), (2, P_SIZE, P_SIZE))
            return lax.dynamic_update_slice(grad_accum, old_block + grad_piece, (zero_index, row_at, col_at))
        grad_total = lax.fori_loop(0, CAP, add_own, grad_total)
        updated_flat = updated_b.reshape(2 * CAP, pixels)
        new_block = project_weights(updated_flat, basis_flat, CAP, K, pixels)
        mode_total = mode_total + jnp.dot(gather_mixing(wt_block), updated_flat, preferred_element_type=jnp.float32)
        return ((grad_total, mode_total), new_block)
    init = (jnp.zeros(object_field.shape, jnp.float32), jnp.zeros((2 * K, pixels), jnp.float32))
    scanned = (jnp.arange(devices, dtype=jnp.int32), weights_dev, amp_dev, slot_count, owner_dev, row_dev, col_dev)
    (grad_total, mode_total), new_blocks = lax.scan(per_device, init, scanned)
    new_object = object_field + OBJ_STEP * grad_total
    new_weights = new_blocks.transpose(1, 0, 2, 3).reshape(2, devices * CAP, K)
    summed = mode_total.reshape(2, K, pixels)
    gram_real, gram_imag = mode_gram(summed[0], summed[1])
    fac_real, fac_imag = cholesky_factor(gram_real, gram_imag)
    new_modes = solve_rows(summed[0], summed[1], fac_real, fac_imag) * math.sqrt(pixels)
    return (new_object, new_modes, new_weights)
```

```python
import math

import jax
import jax.numpy as jnp
import numpy as np
from jax import lax
from jax.experimental import pallas as pl
from jax.experimental.pallas import tpu as pltpu
from jax.sharding import PartitionSpec as P

OBJ_STEP = 0.125
PROBE_STEP = 0.5
RB = 16
f32 = jnp.float32
bf16 = jnp.bfloat16
HI = lax.Precision.HIGHEST


def transform_tables(length):
    ids = np.arange(length)
    angles = (ids[:, None] * ids[None, :] % length) * (2.0 * math.pi / length)
    cos_tab = np.cos(angles) / math.sqrt(length)
    sin_tab = np.sin(angles) / math.sqrt(length)
    forward = np.block([[cos_tab, sin_tab], [-sin_tab, cos_tab]])
    inverse = np.block([[cos_tab, -sin_tab], [sin_tab, cos_tab]])
    return jnp.asarray(forward, dtype=bf16), jnp.asarray(inverse, dtype=bf16)


def iota(shape, dim):
    return lax.broadcasted_iota(jnp.int32, shape, dim)


def widen_kernel(tab_ref, out_ref):
    rows, cols = tab_ref.shape[1:]
    tall, wide = out_ref.shape[1:]
    up = (iota((tall, rows), 0) // RB == iota((tall, rows), 1)).astype(bf16)
    across = (iota((cols, wide), 1) // RB == iota((cols, wide), 0)).astype(bf16)
    same = iota((tall, wide), 0) % RB == iota((tall, wide), 1) % RB
    for at in range(tab_ref.shape[0]):
        left = jnp.dot(up, tab_ref[at], preferred_element_type=f32).astype(bf16)
        full = jnp.dot(left, across, preferred_element_type=f32)
        out_ref[at] = jnp.where(same, full, 0.0).astype(bf16)


def widen(tables):
    count, rows, cols = tables.shape
    return pl.pallas_call(
        widen_kernel,
        out_shape=jax.ShapeDtypeStruct((count, rows * RB, cols * RB), bf16),
        compiler_params=pltpu.CompilerParams(vmem_limit_bytes=32 << 20),
        cost_estimate=pl.CostEstimate(flops=1 << 28, bytes_accessed=1 << 20, transcendentals=0),
        name="widen",
    )(tables)


def cut_kernel(sel_ref, row_ref, col_ref, obj_ref, out_ref):
    spot = pl.program_id(0)
    length = out_ref.shape[2]
    height, width = obj_ref.shape[2:]
    row_at, col_at, sel = row_ref[spot], col_ref[spot], sel_ref[spot]
    rows = (iota((length, height), 1) == iota((length, height), 0) + row_at).astype(bf16)
    cols = (iota((width, length), 0) == iota((width, length), 1) + col_at).astype(bf16)
    for part in range(2):
        band = jnp.dot(rows, obj_ref[sel, part], preferred_element_type=f32).astype(bf16)
        out_ref[0, part] = jnp.dot(band, cols, preferred_element_type=f32).astype(bf16)


def cut_patches(obj_pair, sel, row_at, col_at, length):
    cap = sel.shape[0]
    grid_spec = pltpu.PrefetchScalarGridSpec(
        num_scalar_prefetch=3,
        grid=(cap,),
        in_specs=[pl.BlockSpec(obj_pair.shape, lambda i, *_: (0, 0, 0, 0))],
        out_specs=pl.BlockSpec((1, 2, length, length), lambda i, *_: (i, 0, 0, 0)),
    )
    return pl.pallas_call(
        cut_kernel,
        grid_spec=grid_spec,
        out_shape=jax.ShapeDtypeStruct((cap, 2, length, length), bf16),
        compiler_params=pltpu.CompilerParams(vmem_limit_bytes=32 << 20),
        cost_estimate=pl.CostEstimate(flops=4 << 30, bytes_accessed=4 << 20, transcendentals=0),
        name="cut_patches",
    )(sel, row_at, col_at, obj_pair)


def relax_kernel(tab_ref, meta_ref, mix_ref, *refs):
    blocks = refs[:-8]
    patch_ref, amp_ref, fwd_ref, inv_ref, upd0_ref, upd1_ref, grad_ref, probe_ref = refs[-8:]
    spot = pl.program_id(0)
    length = patch_ref.shape[2]
    half = len(blocks) // 2

    @pl.when(spot == 0)
    def _():
        mix = mix_ref[0]
        for j, block_ref in enumerate(blocks):
            block = block_ref[...].reshape(block_ref.shape[0] * RB, length)
            mixed = jnp.dot(mix, block, preferred_element_type=f32)
            side = meta_ref[1] if j < half else 1 - meta_ref[1]
            at = pl.multiple_of((2 * tab_ref[j] + side) * RB, RB)
            probe_ref[:, pl.ds(at, RB), :] = mixed.reshape(mixed.shape[0] // RB, RB, length)

    live = (spot < meta_ref[0]).astype(f32)
    probe_r, probe_i = probe_ref[2 * spot], probe_ref[2 * spot + 1]
    obj_r, obj_i = patch_ref[0, 0].astype(f32), patch_ref[0, 1].astype(f32)
    exit_r = (probe_r * obj_r - probe_i * obj_i).astype(bf16)
    exit_i = (probe_r * obj_i + probe_i * obj_r).astype(bf16)
    stacked = jnp.concatenate([exit_r, exit_i], axis=0)
    section = jnp.dot(fwd_ref[...], stacked, preferred_element_type=f32).astype(bf16)
    section = jnp.concatenate([section[:length], section[length:]], axis=1)
    far = jnp.dot(section, inv_ref[...], preferred_element_type=f32)
    far_r, far_i = far[:, :length], far[:, length:]
    scale = amp_ref[0].astype(f32) * lax.rsqrt(far_r * far_r + far_i * far_i + 1.0)
    revised = jnp.concatenate([(far_r * scale).astype(bf16), (far_i * scale).astype(bf16)], axis=0)
    back = jnp.dot(inv_ref[...], revised, preferred_element_type=f32).astype(bf16)
    back = jnp.concatenate([back[:length], back[length:]], axis=1)
    near = jnp.dot(back, fwd_ref[...], preferred_element_type=f32)
    delta_r = near[:, :length] - exit_r.astype(f32)
    delta_i = near[:, length:] - exit_i.astype(f32)
    grad_ref[0, 0] = ((probe_r * delta_r + probe_i * delta_i) * live).astype(bf16)
    grad_ref[0, 1] = ((probe_r * delta_i - probe_i * delta_r) * live).astype(bf16)
    change_r = obj_r * delta_r + obj_i * delta_i
    change_i = obj_r * delta_i - obj_i * delta_r
    new_r = ((probe_r + PROBE_STEP * change_r) * live).astype(bf16)
    new_i = ((probe_i + PROBE_STEP * change_i) * live).astype(bf16)
    flip = meta_ref[1] > 0
    for part, value in ((0, new_r), (1, new_i)):
        rows = value.reshape(half, 2, RB, length)
        even, odd = rows[:, 0], rows[:, 1]
        upd0_ref[:, part] = jnp.where(flip, odd, even)
        upd1_ref[:, part] = jnp.where(flip, even, odd)


def whole(arr):
    return pl.BlockSpec(arr.shape, lambda *_: (0,) * arr.ndim)


def relax(tab, meta, mix, blocks, patches, amplitude, forward, inverse):
    cap, _, length, _ = patches.shape
    half = len(blocks) // 2
    plane = pl.BlockSpec((1, 2, length, length), lambda i, *_: (i, 0, 0, 0))
    strip = pl.BlockSpec((half, 2, RB, length), lambda i, *_: (0, i, 0, 0))
    grid_spec = pltpu.PrefetchScalarGridSpec(
        num_scalar_prefetch=2,
        grid=(cap,),
        in_specs=[
            whole(mix), *[whole(block) for block in blocks], plane,
            pl.BlockSpec((1, length, length), lambda i, *_: (i, 0, 0)),
            whole(forward), whole(inverse),
        ],
        out_specs=[strip, strip, plane],
        scratch_shapes=[pltpu.VMEM((2 * cap, length, length), f32)],
    )
    strips = jax.ShapeDtypeStruct((half, 2 * cap, RB, length), bf16)
    return pl.pallas_call(
        relax_kernel,
        grid_spec=grid_spec,
        out_shape=[strips, strips, jax.ShapeDtypeStruct((cap, 2, length, length), bf16)],
        compiler_params=pltpu.CompilerParams(vmem_limit_bytes=48 << 20),
        cost_estimate=pl.CostEstimate(flops=8 << 30, bytes_accessed=16 << 20, transcendentals=1 << 19),
        name="relax_positions",
    )(tab, meta, mix, *blocks, patches, amplitude, forward, inverse)


def settle_kernel(sel_ref, row_ref, col_ref, grad_ref, mine_ref, other_ref):
    spot = pl.program_id(0)
    length = grad_ref.shape[2]
    height, width = mine_ref.shape[1:]
    row_at, col_at, sel = row_ref[spot], col_ref[spot], sel_ref[spot]

    @pl.when(spot == 0)
    def _():
        mine_ref[...] = jnp.zeros_like(mine_ref)
        other_ref[...] = jnp.zeros_like(other_ref)

    cols = (iota((length, width), 1) == iota((length, width), 0) + col_at).astype(bf16)
    rows = (iota((height, length), 0) == iota((height, length), 1) + row_at).astype(bf16)

    def put(ref):
        for part in range(2):
            band = jnp.dot(grad_ref[0, part], cols, preferred_element_type=f32).astype(bf16)
            ref[part] += jnp.dot(rows, band, preferred_element_type=f32)

    @pl.when(sel == 0)
    def _():
        put(mine_ref)

    @pl.when(sel != 0)
    def _():
        put(other_ref)


def settle(sel, row_at, col_at, grads, height, width):
    cap, _, length, _ = grads.shape
    tile = pl.BlockSpec((2, height, width), lambda i, *_: (0, 0, 0))
    grid_spec = pltpu.PrefetchScalarGridSpec(
        num_scalar_prefetch=3,
        grid=(cap,),
        in_specs=[pl.BlockSpec((1, 2, length, length), lambda i, *_: (i, 0, 0, 0))],
        out_specs=[tile, tile],
    )
    shape = jax.ShapeDtypeStruct((2, height, width), f32)
    return pl.pallas_call(
        settle_kernel,
        grid_spec=grid_spec,
        out_shape=[shape, shape],
        compiler_params=pltpu.CompilerParams(vmem_limit_bytes=48 << 20),
        cost_estimate=pl.CostEstimate(flops=4 << 30, bytes_accessed=4 << 20, transcendentals=0),
        name="settle",
    )(sel, row_at, col_at, grads)


def weights_kernel(tab_ref, upd0_ref, upd1_ref, *refs):
    blocks, nw_ref = refs[:-1], refs[-1]
    half = len(blocks) // 2
    lanes = upd0_ref.shape[3]
    tall = upd0_ref.shape[1] * RB
    wide = blocks[0].shape[0] * RB
    table = jnp.zeros((tall, wide), f32)
    for j, block_ref in enumerate(blocks):
        side = upd0_ref if j < half else upd1_ref
        mine = side[tab_ref[j]].reshape(tall, lanes)
        table += lax.dot_general(mine, block_ref[...].reshape(wide, lanes),
                                 (((1,), (1,)), ((), ())), preferred_element_type=f32)
    same = (iota((tall, wide), 0) % RB) == (iota((tall, wide), 1) % RB)
    table = jnp.where(same, table, 0.0)
    slots, modes = tall // (2 * RB), wide // (2 * RB)

    def mul(left, right):
        return jnp.dot(left, right, precision=HI, preferred_element_type=f32)

    def gather_rows(which):
        pick = iota((slots, tall), 1) // RB == 2 * iota((slots, tall), 0) + which
        return mul(pick.astype(f32), table)

    def pick_cols(which):
        pick = iota((wide, modes), 0) // RB == which * modes + iota((wide, modes), 1)
        return pick.astype(f32)

    low, high = gather_rows(0), gather_rows(1)
    cols_r, cols_i = pick_cols(0), pick_cols(1)
    norm = 1.0 / (2 * half * RB * lanes)
    nw_ref[0] = (mul(low, cols_r) + mul(high, cols_i)) * norm
    nw_ref[1] = (mul(high, cols_r) - mul(low, cols_i)) * norm


def new_weights_of(tab, upd0, upd1, blocks):
    grid_spec = pltpu.PrefetchScalarGridSpec(
        num_scalar_prefetch=1,
        grid=(1,),
        in_specs=[whole(upd0), whole(upd1), *[whole(block) for block in blocks]],
        out_specs=pl.BlockSpec((2, upd0.shape[1] // 2, blocks[0].shape[0] // 2), lambda *_: (0, 0, 0)),
    )
    return pl.pallas_call(
        weights_kernel,
        grid_spec=grid_spec,
        out_shape=jax.ShapeDtypeStruct((2, upd0.shape[1] // 2, blocks[0].shape[0] // 2), f32),
        compiler_params=pltpu.CompilerParams(vmem_limit_bytes=48 << 20),
        cost_estimate=pl.CostEstimate(flops=2 << 30, bytes_accessed=6 << 20, transcendentals=0),
        name="new_weights",
    )(tab, upd0, upd1, *blocks)


def sums_kernel(at_ref, wide_ref, near_ref, twin_ref, far_ref, out_ref):
    lanes = near_ref.shape[-1]

    def flat(value):
        return value.reshape(-1, lanes)

    total = jnp.dot(wide_ref[0], flat(near_ref[0]), preferred_element_type=f32)
    total += jnp.dot(wide_ref[1], flat(twin_ref[0]), preferred_element_type=f32)
    total += jnp.dot(wide_ref[2], flat(far_ref[0]), preferred_element_type=f32)
    total += jnp.dot(wide_ref[3], flat(far_ref[1]), preferred_element_type=f32)
    out_ref[...] = total.reshape(out_ref.shape).astype(out_ref.dtype)


def pair_sums(at, wide, near, twin, far, kind):
    lanes = near.shape[-1]
    strip = pl.BlockSpec((1,) + near.shape[1:], lambda i, at: (at[0], 0, 0, 0))
    tall = wide.shape[1] // RB
    grid_spec = pltpu.PrefetchScalarGridSpec(
        num_scalar_prefetch=1,
        grid=(1,),
        in_specs=[whole(wide), strip, strip, whole(far)],
        out_specs=pl.BlockSpec((tall, RB, lanes), lambda *_: (0, 0, 0)),
    )
    return pl.pallas_call(
        sums_kernel,
        grid_spec=grid_spec,
        out_shape=jax.ShapeDtypeStruct((tall, RB, lanes), kind),
        compiler_params=pltpu.CompilerParams(vmem_limit_bytes=16 << 20),
        cost_estimate=pl.CostEstimate(flops=1 << 29, bytes_accessed=2 << 20, transcendentals=0),
        name="mode_sums",
    )(at.reshape(1), wide, near, twin, far)


def finish_kernel(*refs):
    own_ref, others = refs[0], refs[1:-3]
    sum_ref, gram_ref, acc_ref = refs[-3:]
    lanes = own_ref.shape[-1]
    total = own_ref[...]
    for other in others:
        total = total + other[...].astype(f32)
    acc_ref[...] = total
    for row in range(RB):
        sum_ref[:, row * lanes:(row + 1) * lanes] = acc_ref[:, row, :]
    modes = sum_ref.shape[0] // 2
    flat = sum_ref[...]
    full = lax.dot_general(flat, flat, (((1,), (1,)), ((), ())), precision=HI,
                           preferred_element_type=f32)
    gram_ref[0] = full[:modes, :modes] + full[modes:, modes:]
    gram_ref[1] = full[modes:, :modes] - full[:modes, modes:]


def finish_sums(own, others):
    tall, _, lanes = own.shape
    return pl.pallas_call(
        finish_kernel,
        out_shape=[
            jax.ShapeDtypeStruct((tall, RB * lanes), f32),
            jax.ShapeDtypeStruct((2, tall // 2, tall // 2), f32),
        ],
        scratch_shapes=[pltpu.VMEM((tall, RB, lanes), f32)],
        compiler_params=pltpu.CompilerParams(vmem_limit_bytes=16 << 20),
        cost_estimate=pl.CostEstimate(flops=1 << 28, bytes_accessed=2 << 20, transcendentals=0),
        name="finish_sums",
    )(own, *others)


def modes_kernel(norm, gram_ref, sum_ref, out_ref):
    count = gram_ref.shape[1]
    gram_r, gram_i = gram_ref[0], gram_ref[1]
    eye = (iota((count, count), 0) == iota((count, count), 1)).astype(f32)
    zero = jnp.zeros((count, count), f32)
    work = jnp.concatenate([gram_r, gram_i, eye, zero], axis=1)
    turned = jnp.concatenate([-gram_i, gram_r, zero, eye], axis=1)
    row_ids = iota((count, 1), 0)
    roots = jnp.zeros((count, 1), f32)
    for pivot in range(count):
        lead = work[pivot:pivot + 1, pivot:pivot + 1]
        roots = jnp.where(row_ids == pivot, lead, roots)
        if pivot + 1 < count:
            below = jnp.where(row_ids > pivot, 1.0 / lead, 0.0)
            coef_r = work[:, pivot:pivot + 1] * below
            coef_i = work[:, count + pivot:count + pivot + 1] * below
            row, row_t = work[pivot:pivot + 1], turned[pivot:pivot + 1]
            work = work - (coef_r * row + coef_i * row_t)
            turned = turned - (coef_r * row_t - coef_i * row)
    back = work[:, 2 * count:] * (norm * lax.rsqrt(roots))
    back_r, back_i = back[:, :count], back[:, count:]
    full = jnp.concatenate([
        jnp.concatenate([back_r, -back_i], axis=1),
        jnp.concatenate([back_i, back_r], axis=1)], axis=0)
    out_ref[...] = jnp.dot(full, sum_ref[...], precision=HI, preferred_element_type=f32)


def new_modes_of(gram, summed, norm):
    def kernel(gram_ref, sum_ref, out_ref):
        modes_kernel(norm, gram_ref, sum_ref, out_ref)

    return pl.pallas_call(
        kernel,
        out_shape=jax.ShapeDtypeStruct(summed.shape, f32),
        compiler_params=pltpu.CompilerParams(vmem_limit_bytes=32 << 20),
        cost_estimate=pl.CostEstimate(flops=1 << 27, bytes_accessed=1 << 20, transcendentals=256),
        name="orthonormal_modes",
    )(gram, summed)


def swap_tiles(value):
    count = lax.axis_size("tile")
    return lax.ppermute(value, "tile", [(i, (i + 1) % count) for i in range(count)])


def turn(value, step):
    count = lax.axis_size("scan")
    return lax.ppermute(value, "scan", [(i, (i + 2 * step) % count) for i in range(count)])


def across(value):
    count = lax.axis_size("scan")
    return lax.ppermute(value, "scan", [(i, i ^ 1) for i in range(count)])


def gather_blocks(own):
    scan = lax.axis_index("scan")
    z, y = scan // 2, scan % 2
    come = {step: turn(own, step) for step in (2, 1, 3)}
    row = [own] + [come[step] for step in (2, 1, 3)]
    side = [across(value) for value in row]
    mine = row + side
    other = [swap_tiles(value) for value in mine]
    order = jnp.stack([z, (z + 2) % 4, (z + 3) % 4, (z + 1) % 4])
    tab = jnp.concatenate([2 * order + y, 2 * order + 1 - y])
    return mine + other, jnp.concatenate([tab, tab])


def gather_any(own):
    rows = own.shape[1]
    every = lax.all_gather(own, ("scan", "tile"))
    every = every.reshape((-1, RB // rows) + own.shape).transpose(0, 2, 1, 3, 4)
    every = every.reshape(-1, own.shape[0], RB, own.shape[2])
    half = every.shape[0] // 2
    tab = jnp.arange(half, dtype=jnp.int32)
    return [every[i] for i in (*range(0, 2 * half, 2), *range(1, 2 * half, 2))], jnp.concatenate([tab, tab])


def gather_mixing(weights_b):
    wt_r, wt_i = jnp.swapaxes(weights_b[0], 0, 1), jnp.swapaxes(weights_b[1], 0, 1)
    real_rows = jnp.stack([wt_r, wt_i], axis=2)
    imag_rows = jnp.stack([-wt_i, wt_r], axis=2)
    count, cap = wt_r.shape
    return jnp.stack([real_rows, imag_rows], axis=0).reshape(2 * count, 2 * cap)


def scatter_sums(weights_b, upd0, upd1):
    scan = lax.axis_index("scan")
    z, y = scan // 2, scan % 2
    pair = jnp.stack([weights_b, swap_tiles(weights_b)])
    quad = jnp.concatenate([pair, across(pair)])
    wide = widen(jax.vmap(gather_mixing)(quad))
    twin = swap_tiles(upd1)
    far = {}
    for step in (2, 1, 3, 0):
        at = 2 * ((z + step) % 4) + 1 - y
        far[step] = across(jnp.stack([
            lax.dynamic_index_in_dim(upd0, at, 0, keepdims=False),
            lax.dynamic_index_in_dim(twin, at, 0, keepdims=False)]))
    come = []
    for step in (2, 1, 3):
        part = pair_sums(2 * ((z + step) % 4) + y, wide, upd0, twin, far[step], bf16)
        come.append(turn(part, step))
    own = pair_sums(2 * z + y, wide, upd0, twin, far[0], f32)
    return finish_sums(own, come)


def scatter_any(weights_b, upd0, upd1):
    devices = lax.axis_size("scan") * lax.axis_size("tile")
    half, slots, _, length = upd0.shape
    every = lax.all_gather(weights_b, ("scan", "tile"))
    rows = 2 * half * RB // devices
    parts = jnp.stack([upd0, upd1], axis=1).reshape(2 * half, slots, RB // rows, rows, length)
    parts = parts.transpose(0, 2, 1, 3, 4).reshape(devices, slots, rows, length)
    arrived = lax.all_to_all(parts, ("scan", "tile"), split_axis=0, concat_axis=0, tiled=True)
    flat = arrived.reshape(devices, slots // 2, 2, rows * length).astype(f32)
    wt_r, wt_i = every[:, 0].astype(f32), every[:, 1].astype(f32)
    up_r, up_i = flat[:, :, 0], flat[:, :, 1]

    def mul(left, right):
        return jnp.einsum("dpk,dpx->kx", left, right, precision=HI)

    sum_r = mul(wt_r, up_r) + mul(wt_i, up_i)
    sum_i = mul(wt_r, up_i) - mul(wt_i, up_r)

    def pair(left, right):
        return jnp.dot(left, right.T, precision=HI)

    gram = jnp.stack([pair(sum_r, sum_r) + pair(sum_i, sum_i),
                      pair(sum_i, sum_r) - pair(sum_r, sum_i)])
    return jnp.concatenate([sum_r, sum_i]), gram


def sum_everywhere(value):
    value = value + swap_tiles(value)
    count = lax.axis_size("scan")
    step = 1
    while step < count:
        value = value + lax.ppermute(value, "scan", [(i, i ^ step) for i in range(count)])
        step *= 2
    return value


def local(
    object_field, probe_modes, weights, amplitude, slot_count, tile_owner, corner_row, corner_col
):
    n_tile = lax.axis_size("tile")
    devices = lax.axis_size("scan") * n_tile
    tile = lax.axis_index("tile")
    cap, length, _ = amplitude.shape
    count = probe_modes.shape[1]
    pixels = length * length
    rows = length // devices
    forward, inverse = transform_tables(length)

    def mine(value):
        return lax.dynamic_slice_in_dim(value, tile * cap, cap)

    owner, row_at, col_at = mine(tile_owner), mine(corner_row), mine(corner_col)
    sel = jnp.where(owner == tile, 0, 1).astype(jnp.int32)
    live_n = lax.dynamic_index_in_dim(slot_count, tile, 0, keepdims=False)

    own = probe_modes.astype(bf16).reshape(2 * count, rows, length)
    obj_b = object_field.astype(bf16)
    obj_pair = jnp.stack([obj_b, swap_tiles(obj_b)])
    weights_b = weights.astype(bf16)
    planned = lax.axis_size("scan") == 8 and n_tile == 2 and rows == RB
    blocks, tab = gather_blocks(own) if planned else gather_any(own)
    patches = cut_patches(obj_pair, sel, row_at, col_at, length)

    wt_r, wt_i = weights_b[0], weights_b[1]
    mix = jnp.stack([jnp.concatenate([wt_r, -wt_i], axis=1),
                     jnp.concatenate([wt_i, wt_r], axis=1)], axis=1)
    mix = widen(mix.reshape(1, 2 * cap, 2 * count))
    meta = jnp.stack([live_n, tile if planned else jnp.zeros_like(tile)])
    upd0, upd1, grads = relax(tab, meta, mix, blocks, patches, amplitude, forward, inverse)

    summed, gram = (scatter_sums if planned else scatter_any)(weights_b, upd0, upd1)
    mine_sum, other_sum = settle(sel, row_at, col_at, grads, *object_field.shape[1:])
    new_object = object_field + OBJ_STEP * (mine_sum + swap_tiles(other_sum))
    new_weights = new_weights_of(tab, upd0, upd1, blocks)
    gram = sum_everywhere(gram)
    new_modes = new_modes_of(gram, summed, math.sqrt(pixels)).reshape(probe_modes.shape)
    return (new_object, new_modes, new_weights)


def solution(mesh):
    in_specs = (
        P(None, ("groups", "scan", "tile"), None),
        P(None, "groups", ("scan", "tile")),
        P(None, ("groups", "scan", "tile"), None),
        P(("groups", "scan", "tile"), None, None),
        P(("groups", "scan")),
        P(("groups", "scan")),
        P(("groups", "scan")),
        P(("groups", "scan")),
    )
    out_specs = (
        P(None, ("groups", "scan", "tile"), None),
        P(None, "groups", ("scan", "tile")),
        P(None, ("groups", "scan", "tile"), None),
    )
    return jax.shard_map(local, mesh=mesh, in_specs=in_specs, out_specs=out_specs, check_vma=False)
```

```python
import math

import jax
import jax.numpy as jnp
import numpy as np
from jax import lax
from jax.experimental import pallas as pl
from jax.experimental.pallas import tpu as pltpu
from jax.sharding import PartitionSpec as P

OBJ_STEP = 0.125
PROBE_STEP = 0.5
RB = 16
f32 = jnp.float32
bf16 = jnp.bfloat16
HI = lax.Precision.HIGHEST


def transform_tables(length):
    ids = np.arange(length)
    angles = (ids[:, None] * ids[None, :] % length) * (2.0 * math.pi / length)
    cos_tab = np.cos(angles) / math.sqrt(length)
    sin_tab = np.sin(angles) / math.sqrt(length)
    forward = np.block([[cos_tab, sin_tab], [-sin_tab, cos_tab]])
    inverse = np.block([[cos_tab, -sin_tab], [sin_tab, cos_tab]])
    return jnp.asarray(forward, dtype=bf16), jnp.asarray(inverse, dtype=bf16)


def iota(shape, dim):
    return lax.broadcasted_iota(jnp.int32, shape, dim)


def widen_kernel(tab_ref, out_ref):
    rows, cols = tab_ref.shape[1:]
    tall, wide = out_ref.shape[1:]
    up = (iota((tall, rows), 0) // RB == iota((tall, rows), 1)).astype(bf16)
    across = (iota((cols, wide), 1) // RB == iota((cols, wide), 0)).astype(bf16)
    same = iota((tall, wide), 0) % RB == iota((tall, wide), 1) % RB
    for at in range(tab_ref.shape[0]):
        left = jnp.dot(up, tab_ref[at], preferred_element_type=f32).astype(bf16)
        full = jnp.dot(left, across, preferred_element_type=f32)
        out_ref[at] = jnp.where(same, full, 0.0).astype(bf16)


def widen(tables):
    count, rows, cols = tables.shape
    return pl.pallas_call(
        widen_kernel,
        out_shape=jax.ShapeDtypeStruct((count, rows * RB, cols * RB), bf16),
        compiler_params=pltpu.CompilerParams(vmem_limit_bytes=8 << 20),
        cost_estimate=pl.CostEstimate(flops=1 << 28, bytes_accessed=1 << 20, transcendentals=0),
        name="widen",
    )(tables)


def cut_kernel(sel_ref, row_ref, col_ref, obj_ref, out_ref):
    spot = pl.program_id(0)
    length = out_ref.shape[2]
    height, width = obj_ref.shape[2:]
    row_at, col_at, sel = row_ref[spot], col_ref[spot], sel_ref[spot]
    rows = (iota((length, height), 1) == iota((length, height), 0) + row_at).astype(bf16)
    cols = (iota((width, length), 0) == iota((width, length), 1) + col_at).astype(bf16)
    for part in range(2):
        band = jnp.dot(rows, obj_ref[sel, part], preferred_element_type=f32).astype(bf16)
        out_ref[0, part] = jnp.dot(band, cols, preferred_element_type=f32).astype(bf16)


def cut_patches(obj_pair, sel, row_at, col_at, length):
    cap = sel.shape[0]
    grid_spec = pltpu.PrefetchScalarGridSpec(
        num_scalar_prefetch=3,
        grid=(cap,),
        in_specs=[pl.BlockSpec(obj_pair.shape, lambda i, *_: (0, 0, 0, 0))],
        out_specs=pl.BlockSpec((1, 2, length, length), lambda i, *_: (i, 0, 0, 0)),
    )
    return pl.pallas_call(
        cut_kernel,
        grid_spec=grid_spec,
        out_shape=jax.ShapeDtypeStruct((cap, 2, length, length), bf16),
        compiler_params=pltpu.CompilerParams(vmem_limit_bytes=12 << 20),
        cost_estimate=pl.CostEstimate(flops=4 << 30, bytes_accessed=4 << 20, transcendentals=0),
        name="cut_patches",
    )(sel, row_at, col_at, obj_pair)


STEPS = (0, 2, 3, 1)


def relax_kernel(tab_ref, live_ref, mix_ref, *refs):
    count = len(STEPS)
    blocks, refs = refs[:4 * count], refs[4 * count:]
    patch_ref, amp_ref, fwd_ref, inv_ref, keep0_ref, keep1_ref = refs[:6]
    cross0, cross1 = refs[6:6 + count], refs[6 + count:6 + 2 * count]
    grad_ref, stash_ref, probe_ref, new_ref = refs[6 + 2 * count:]
    group = pl.program_id(0)
    each = patch_ref.shape[0]
    length = patch_ref.shape[2]

    @pl.when(group == 0)
    def _():
        mix = mix_ref[0]
        for j, block_ref in enumerate(blocks):
            block = block_ref[...].reshape(block_ref.shape[0] * RB, length)
            mixed = jnp.dot(mix, block, preferred_element_type=f32)
            at = pl.multiple_of(tab_ref[j] * RB, RB)
            probe_ref[:, pl.ds(at, RB), :] = mixed.reshape(mixed.shape[0] // RB, RB, length)

    share = stash_ref.shape[0]
    for turn_at in range(len(blocks) // share):
        @pl.when(group == turn_at)
        def _(turn_at=turn_at):
            for i in range(share):
                stash_ref[i] = blocks[share * turn_at + i][...]

    def planes(q):
        spot = each * group + q
        return (probe_ref[2 * spot], probe_ref[2 * spot + 1],
                patch_ref[q, 0].astype(f32), patch_ref[q, 1].astype(f32))

    def leave(q):
        probe_r, probe_i, obj_r, obj_i = planes(q)
        exit_r = (probe_r * obj_r - probe_i * obj_i).astype(bf16)
        exit_i = (probe_r * obj_i + probe_i * obj_r).astype(bf16)
        return exit_r, exit_i

    def rows_pass(table, pairs):
        both = jnp.concatenate([jnp.concatenate(pair, axis=0) for pair in pairs], axis=1)
        out = jnp.dot(table[...], both, preferred_element_type=f32).astype(bf16)
        return jnp.concatenate([
            jnp.concatenate([out[:length, q * length:(q + 1) * length],
                             out[length:, q * length:(q + 1) * length]], axis=1)
            for q in range(each)], axis=0)

    def cols_pass(table, value):
        out = jnp.dot(value, table[...], preferred_element_type=f32)
        return [out[q * length:(q + 1) * length] for q in range(each)]

    def revise(q, far):
        far_r, far_i = far[:, :length], far[:, length:]
        scale = amp_ref[q].astype(f32) * lax.rsqrt(far_r * far_r + far_i * far_i + 1.0)
        return (far_r * scale).astype(bf16), (far_i * scale).astype(bf16)

    def update(q, exits, near):
        live = (each * group + q < live_ref[0]).astype(f32)
        probe_r, probe_i, obj_r, obj_i = planes(q)
        delta_r = near[:, :length] - exits[0].astype(f32)
        delta_i = near[:, length:] - exits[1].astype(f32)
        grad_ref[q, 0] = ((probe_r * delta_r + probe_i * delta_i) * live).astype(bf16)
        grad_ref[q, 1] = ((probe_r * delta_i - probe_i * delta_r) * live).astype(bf16)
        change_r = obj_r * delta_r + obj_i * delta_i
        change_i = obj_r * delta_i - obj_i * delta_r
        for part, value in ((0, probe_r + PROBE_STEP * change_r), (1, probe_i + PROBE_STEP * change_i)):
            new_ref[2 * q + part] = (value * live).astype(bf16).reshape(4 * count, RB, length)

    exits = [leave(q) for q in range(each)]
    far = cols_pass(inv_ref, rows_pass(fwd_ref, exits))
    revised = [revise(q, far[q]) for q in range(each)]
    near = cols_pass(fwd_ref, rows_pass(inv_ref, revised))
    for q in range(each):
        update(q, exits[q], near[q])
    for j in range(4 * count):
        at = tab_ref[j]
        side, far_side, place = j // (2 * count), j // count % 2, j % count
        for row in range(2 * each):
            if far_side:
                (cross1 if side else cross0)[place][row] = new_ref[row, at]
            else:
                (keep1_ref if side else keep0_ref)[place, row] = new_ref[row, at]


def whole(arr):
    return pl.BlockSpec(arr.shape, lambda *_: (0,) * arr.ndim)


def relax(tab, live, mix, blocks, patches, amplitude, forward, inverse):
    cap, _, length, _ = patches.shape
    count = len(STEPS)
    each = 4 if cap % 4 == 0 else 1
    share = len(blocks) * each // cap
    plane = pl.BlockSpec((each, 2, length, length), lambda i, *_: (i, 0, 0, 0))
    strips = pl.BlockSpec((count, 2 * each, RB, length), lambda i, *_: (0, i, 0, 0))
    strip = pl.BlockSpec((2 * each, RB, length), lambda i, *_: (i, 0, 0))
    grid_spec = pltpu.PrefetchScalarGridSpec(
        num_scalar_prefetch=2,
        grid=(cap // each,),
        in_specs=[
            whole(mix), *[whole(block) for block in blocks], plane,
            pl.BlockSpec((each, length, length), lambda i, *_: (i, 0, 0)),
            whole(forward), whole(inverse),
        ],
        out_specs=[strips, strips, *[strip] * (2 * count), plane,
                   pl.BlockSpec((share,) + blocks[0].shape, lambda i, *_: (i, 0, 0, 0))],
        scratch_shapes=[
            pltpu.VMEM((2 * cap, length, length), f32),
            pltpu.VMEM((2 * each, 4 * count, RB, length), bf16),
        ],
    )
    many = jax.ShapeDtypeStruct((count, 2 * cap, RB, length), bf16)
    single = jax.ShapeDtypeStruct((2 * cap, RB, length), bf16)
    outs = pl.pallas_call(
        relax_kernel,
        grid_spec=grid_spec,
        out_shape=[many, many, *[single] * (2 * count),
                   pltpu.HBM((cap, 2, length, length), bf16),
                   pltpu.HBM((len(blocks),) + blocks[0].shape, bf16)],
        compiler_params=pltpu.CompilerParams(vmem_limit_bytes=28 << 20),
        cost_estimate=pl.CostEstimate(flops=8 << 30, bytes_accessed=16 << 20, transcendentals=1 << 19),
        name="relax_positions",
    )(tab, live.reshape(1), mix, *blocks, patches, amplitude, forward, inverse)
    return (outs[0], outs[1], outs[2:2 + count], outs[2 + count:2 + 2 * count]), outs[-2], outs[-1]


def settle_kernel(sel_ref, row_ref, col_ref, grad_ref, mine_ref, other_ref, band_ref):
    cap, _, length, _ = grad_ref.shape
    height, width = mine_ref.shape[1:]
    places = []
    for spot in range(cap):
        row_at, col_at, sel = row_ref[spot], col_ref[spot], sel_ref[spot]
        cols = (iota((length, width), 1) == iota((length, width), 0) + col_at).astype(bf16)
        for part in range(2):
            band = jnp.dot(grad_ref[spot, part], cols, preferred_element_type=f32)
            band_ref[spot * length:(spot + 1) * length, part * width:(part + 1) * width] = band.astype(bf16)
        place = iota((2 * height, length), 1) + row_at + height * sel
        places.append((iota((2 * height, length), 0) == place).astype(bf16))
    places = jnp.concatenate(places, axis=1)
    for part in range(2):
        total = jnp.dot(places, band_ref[:, part * width:(part + 1) * width], preferred_element_type=f32)
        mine_ref[part] = total[:height]
        other_ref[part] = total[height:]


def settle(sel, row_at, col_at, grads, height, width):
    cap, _, length, _ = grads.shape
    tile = pl.BlockSpec((2, height, width), lambda *_: (0, 0, 0))
    grid_spec = pltpu.PrefetchScalarGridSpec(
        num_scalar_prefetch=3,
        grid=(1,),
        in_specs=[whole(grads)],
        out_specs=[tile, tile],
        scratch_shapes=[pltpu.VMEM((cap * length, 2 * width), bf16)],
    )
    shape = jax.ShapeDtypeStruct((2, height, width), f32)
    return pl.pallas_call(
        settle_kernel,
        grid_spec=grid_spec,
        out_shape=[shape, shape],
        compiler_params=pltpu.CompilerParams(vmem_limit_bytes=20 << 20),
        cost_estimate=pl.CostEstimate(flops=4 << 30, bytes_accessed=4 << 20, transcendentals=0),
        name="settle",
    )(sel, row_at, col_at, grads)


def weights_kernel(keep0_ref, keep1_ref, *refs):
    count = len(STEPS)
    cross, (block_ref, nw_ref) = refs[:2 * count], refs[2 * count:]
    lanes = keep0_ref.shape[3]
    tall = keep0_ref.shape[1] * RB
    wide = block_ref.shape[1] * RB
    table = jnp.zeros((tall, wide), f32)
    for j in range(4 * count):
        side, far_side, place = j // (2 * count), j // count % 2, j % count
        if far_side:
            mine = cross[count * side + place][...]
        else:
            mine = (keep1_ref if side else keep0_ref)[place]
        table += lax.dot_general(mine.reshape(tall, lanes), block_ref[j].reshape(wide, lanes),
                                 (((1,), (1,)), ((), ())), preferred_element_type=f32)
    same = (iota((tall, wide), 0) % RB) == (iota((tall, wide), 1) % RB)
    table = jnp.where(same, table, 0.0)
    slots, modes = tall // (2 * RB), wide // (2 * RB)

    def mul(left, right):
        return jnp.dot(left, right, precision=HI, preferred_element_type=f32)

    def gather_rows(which):
        pick = iota((slots, tall), 1) // RB == 2 * iota((slots, tall), 0) + which
        return mul(pick.astype(f32), table)

    def pick_cols(which):
        pick = iota((wide, modes), 0) // RB == which * modes + iota((wide, modes), 1)
        return pick.astype(f32)

    low, high = gather_rows(0), gather_rows(1)
    cols_r, cols_i = pick_cols(0), pick_cols(1)
    norm = 1.0 / (4 * count * RB * lanes)
    nw_ref[0] = (mul(low, cols_r) + mul(high, cols_i)) * norm
    nw_ref[1] = (mul(high, cols_r) - mul(low, cols_i)) * norm


def new_weights_of(updated, blocks):
    keep0, keep1, cross0, cross1 = updated
    args = [keep0, keep1, *cross0, *cross1, blocks]
    return pl.pallas_call(
        weights_kernel,
        out_shape=jax.ShapeDtypeStruct((2, keep0.shape[1] // 2, blocks.shape[1] // 2), f32),
        compiler_params=pltpu.CompilerParams(vmem_limit_bytes=16 << 20),
        cost_estimate=pl.CostEstimate(flops=2 << 30, bytes_accessed=6 << 20, transcendentals=0),
        name="new_weights",
    )(*args)


def sums_kernel(wide_ref, near_ref, twin_ref, far_ref, far_twin_ref, out_ref):
    lanes = near_ref.shape[-1]

    def flat(value):
        return value.reshape(-1, lanes)

    total = jnp.dot(wide_ref[0], flat(near_ref[0]), preferred_element_type=f32)
    total += jnp.dot(wide_ref[1], flat(twin_ref[0]), preferred_element_type=f32)
    total += jnp.dot(wide_ref[2], flat(far_ref[...]), preferred_element_type=f32)
    total += jnp.dot(wide_ref[3], flat(far_twin_ref[...]), preferred_element_type=f32)
    out_ref[...] = total.reshape(out_ref.shape).astype(out_ref.dtype)


def pair_sums(place, wide, near, twin, far, far_twin, kind):
    lanes = near.shape[-1]
    strip = pl.BlockSpec((1,) + near.shape[1:], lambda i: (place, 0, 0, 0))
    tall = wide.shape[1] // RB
    return pl.pallas_call(
        sums_kernel,
        grid=(1,),
        in_specs=[whole(wide), strip, strip, whole(far), whole(far_twin)],
        out_specs=pl.BlockSpec((tall, RB, lanes), lambda *_: (0, 0, 0)),
        out_shape=jax.ShapeDtypeStruct((tall, RB, lanes), kind),
        compiler_params=pltpu.CompilerParams(vmem_limit_bytes=8 << 20),
        cost_estimate=pl.CostEstimate(flops=1 << 29, bytes_accessed=2 << 20, transcendentals=0),
        name="mode_sums",
    )(wide, near, twin, far, far_twin)


def finish_kernel(*refs):
    own_ref, others = refs[0], refs[1:-3]
    sum_ref, gram_ref, acc_ref = refs[-3:]
    lanes = own_ref.shape[-1]
    total = own_ref[...]
    for other in others:
        total = total + other[...].astype(f32)
    acc_ref[...] = total
    for row in range(RB):
        sum_ref[:, row * lanes:(row + 1) * lanes] = acc_ref[:, row, :]
    modes = sum_ref.shape[0] // 2
    flat = sum_ref[...]
    full = lax.dot_general(flat, flat, (((1,), (1,)), ((), ())), precision=HI,
                           preferred_element_type=f32)
    gram_ref[0] = full[:modes, :modes] + full[modes:, modes:]
    gram_ref[1] = full[modes:, :modes] - full[:modes, modes:]


def finish_sums(own, others):
    tall, _, lanes = own.shape
    return pl.pallas_call(
        finish_kernel,
        out_shape=[
            jax.ShapeDtypeStruct((tall, RB * lanes), f32),
            jax.ShapeDtypeStruct((2, tall // 2, tall // 2), f32),
        ],
        scratch_shapes=[pltpu.VMEM((tall, RB, lanes), f32)],
        compiler_params=pltpu.CompilerParams(vmem_limit_bytes=8 << 20),
        cost_estimate=pl.CostEstimate(flops=1 << 28, bytes_accessed=2 << 20, transcendentals=0),
        name="finish_sums",
    )(own, *others)


def modes_kernel(norm, gram_ref, sum_ref, out_ref):
    count = gram_ref.shape[1]
    gram_r, gram_i = gram_ref[0], gram_ref[1]
    eye = (iota((count, count), 0) == iota((count, count), 1)).astype(f32)
    zero = jnp.zeros((count, count), f32)
    work = jnp.concatenate([gram_r, gram_i, eye, zero], axis=1)
    turned = jnp.concatenate([-gram_i, gram_r, zero, eye], axis=1)
    row_ids = iota((count, 1), 0)
    roots = jnp.zeros((count, 1), f32)
    for pivot in range(count):
        lead = work[pivot:pivot + 1, pivot:pivot + 1]
        roots = jnp.where(row_ids == pivot, lead, roots)
        if pivot + 1 < count:
            below = jnp.where(row_ids > pivot, 1.0 / lead, 0.0)
            coef_r = work[:, pivot:pivot + 1] * below
            coef_i = work[:, count + pivot:count + pivot + 1] * below
            row, row_t = work[pivot:pivot + 1], turned[pivot:pivot + 1]
            work = work - (coef_r * row + coef_i * row_t)
            turned = turned - (coef_r * row_t - coef_i * row)
    back = work[:, 2 * count:] * (norm * lax.rsqrt(roots))
    back_r, back_i = back[:, :count], back[:, count:]
    full = jnp.concatenate([
        jnp.concatenate([back_r, -back_i], axis=1),
        jnp.concatenate([back_i, back_r], axis=1)], axis=0)
    out_ref[...] = jnp.dot(full, sum_ref[...], precision=HI, preferred_element_type=f32)


def new_modes_of(gram, summed, norm):
    def kernel(gram_ref, sum_ref, out_ref):
        modes_kernel(norm, gram_ref, sum_ref, out_ref)

    return pl.pallas_call(
        kernel,
        out_shape=jax.ShapeDtypeStruct(summed.shape, f32),
        compiler_params=pltpu.CompilerParams(vmem_limit_bytes=8 << 20),
        cost_estimate=pl.CostEstimate(flops=1 << 27, bytes_accessed=1 << 20, transcendentals=256),
        name="orthonormal_modes",
    )(gram, summed)


def swap_tiles(value):
    count = lax.axis_size("tile")
    return lax.ppermute(value, "tile", [(i, (i + 1) % count) for i in range(count)])


def turn(value, step):
    count = lax.axis_size("scan")
    return lax.ppermute(value, "scan", [(i, (i + 2 * step) % count) for i in range(count)])


def across(value):
    count = lax.axis_size("scan")
    return lax.ppermute(value, "scan", [(i, i ^ 1) for i in range(count)])


def after(value, *others):
    return lax.optimization_barrier((value, *others))[0]


def places(z, y, tile):
    steps = jnp.array(STEPS, jnp.int32)
    strips = 2 * ((z + steps) % len(STEPS))
    strips = jnp.concatenate([strips + y, strips + 1 - y])
    return jnp.concatenate([2 * strips + tile, 2 * strips + 1 - tile]).astype(jnp.int32)


def gather_blocks(own, obj_b, cut, ready):
    come = {1: turn(own, 1), 3: turn(own, 3)}
    side = {0: across(own)}
    obj_pair = jnp.stack([obj_b, swap_tiles(obj_b)])
    patches = cut(obj_pair)
    patches, come[1], come[3], ready = lax.optimization_barrier((patches, come[1], come[3], ready))
    come[2] = turn(come[1], 1)
    for step in (1, 3, 2):
        side[step] = across(come[step])
    come[0] = own
    order = [-step % len(STEPS) for step in STEPS]
    mine = [come[step] for step in order] + [side[step] for step in order]
    return mine + [swap_tiles(value) for value in mine], patches, ready


def gather_any(own, obj_b, cut, ready):
    rows = own.shape[1]
    every = lax.all_gather(own, ("scan", "tile"))
    every = every.reshape((-1, RB // rows) + own.shape).transpose(0, 2, 1, 3, 4)
    every = every.reshape(-1, own.shape[0], RB, own.shape[2])
    blocks = [every[4 * step + 2 * y + tile] for tile in (0, 1) for y in (0, 1) for step in STEPS]
    return blocks, cut(jnp.stack([obj_b, swap_tiles(obj_b)])), ready


def gather_mixing(weights_b):
    wt_r, wt_i = jnp.swapaxes(weights_b[0], 0, 1), jnp.swapaxes(weights_b[1], 0, 1)
    real_rows = jnp.stack([wt_r, wt_i], axis=2)
    imag_rows = jnp.stack([-wt_i, wt_r], axis=2)
    count, cap = wt_r.shape
    return jnp.stack([real_rows, imag_rows], axis=0).reshape(2 * count, 2 * cap)


def scatter_sums(weights_b, updated, blocks):
    keep0, keep1, cross0, cross1 = updated
    pair = jnp.stack([weights_b, swap_tiles(weights_b)])
    pair = after(pair, blocks[-1])
    quad = jnp.concatenate([pair, across(pair)])
    wide = widen(jax.vmap(gather_mixing)(quad))
    order = (2, 3, 1, 0)
    at = {step: STEPS.index(step) for step in order}
    twin_cross = {step: swap_tiles(cross1[at[step]]) for step in order}
    twin = swap_tiles(keep1)
    far, far_twin, line = {}, {}, []
    for step in order:
        for value, dest in ((cross0[at[step]], far), (twin_cross[step], far_twin)):
            dest[step] = across(after(value, line[-3]) if len(line) >= 3 else value)
            line.append(dest[step])

    def part(step, kind):
        return pair_sums(at[step], wide, keep0, twin, far[step], far_twin[step], kind)

    through = turn(part(2, bf16), 1)
    third = turn(part(3, bf16), 3)
    first = turn((part(1, f32) + through.astype(f32)).astype(bf16), 1)
    return finish_sums(part(0, f32), [first, third])


def scatter_any(weights_b, updated, _):
    devices = lax.axis_size("scan") * lax.axis_size("tile")
    keep0, keep1, cross0, cross1 = updated
    count, slots, _, length = keep0.shape
    every = lax.all_gather(weights_b, ("scan", "tile"))
    rows = 4 * count * RB // devices
    parts = jnp.stack([keep0, keep1, jnp.stack(cross0), jnp.stack(cross1)], axis=1)
    parts = jnp.stack([parts[STEPS.index(step)] for step in range(count)])
    parts = parts.reshape(4 * count, slots, RB // rows, rows, length)
    parts = parts.transpose(0, 2, 1, 3, 4).reshape(devices, slots, rows, length)
    arrived = lax.all_to_all(parts, ("scan", "tile"), split_axis=0, concat_axis=0, tiled=True)
    flat = arrived.reshape(devices, slots // 2, 2, rows * length).astype(f32)
    wt_r, wt_i = every[:, 0].astype(f32), every[:, 1].astype(f32)
    up_r, up_i = flat[:, :, 0], flat[:, :, 1]

    def mul(left, right):
        return jnp.einsum("dpk,dpx->kx", left, right, precision=HI)

    sum_r = mul(wt_r, up_r) + mul(wt_i, up_i)
    sum_i = mul(wt_r, up_i) - mul(wt_i, up_r)

    def pair(left, right):
        return jnp.dot(left, right.T, precision=HI)

    gram = jnp.stack([pair(sum_r, sum_r) + pair(sum_i, sum_i),
                      pair(sum_i, sum_r) - pair(sum_r, sum_i)])
    return jnp.concatenate([sum_r, sum_i]), gram


def sum_everywhere(value, works):
    value = value + swap_tiles(value)
    count = lax.axis_size("scan")
    step, works = 1, list(works)
    results = []
    while step < count:
        come = lax.ppermute(value, "scan", [(i, i ^ step) for i in range(count)])
        step *= 2
        if works and step < count:
            results.append(works.pop(0)(value, results))
            value, come, results[-1] = lax.optimization_barrier((value, come, results[-1]))
        value = value + come
    return value, results


def local(
    object_field, probe_modes, weights, amplitude, slot_count, tile_owner, corner_row, corner_col
):
    n_tile = lax.axis_size("tile")
    devices = lax.axis_size("scan") * n_tile
    tile = lax.axis_index("tile")
    cap, length, _ = amplitude.shape
    count = probe_modes.shape[1]
    pixels = length * length
    rows = length // devices
    forward, inverse = transform_tables(length)

    def mine(value):
        return lax.dynamic_slice_in_dim(value, tile * cap, cap)

    owner, row_at, col_at = mine(tile_owner), mine(corner_row), mine(corner_col)
    sel = jnp.where(owner == tile, 0, 1).astype(jnp.int32)
    live_n = lax.dynamic_index_in_dim(slot_count, tile, 0, keepdims=False)

    own = probe_modes.astype(bf16).reshape(2 * count, rows, length)
    obj_b = object_field.astype(bf16)
    weights_b = weights.astype(bf16)
    planned = lax.axis_size("scan") == 8 and n_tile == 2 and rows == RB

    def cut(obj_pair):
        return cut_patches(obj_pair, sel, row_at, col_at, length)

    scan = lax.axis_index("scan")
    tab = places(scan // 2, scan % 2, tile) if planned else places(0, 0, 0)
    wt_r, wt_i = weights_b[0], weights_b[1]
    mix = jnp.stack([jnp.concatenate([wt_r, -wt_i], axis=1),
                     jnp.concatenate([wt_i, wt_r], axis=1)], axis=1)
    mix = widen(mix.reshape(1, 2 * cap, 2 * count))
    blocks, patches, (tab, mix, live_n, forward, inverse) = (gather_blocks if planned else gather_any)(
        own, obj_b, cut, (tab, mix, live_n, forward, inverse))
    updated, grads, stash = relax(tab, live_n, mix, blocks, patches, amplitude, forward, inverse)

    summed, gram = (scatter_sums if planned else scatter_any)(weights_b, updated, blocks)

    def put_back(token, _):
        mine_sum, other_sum = settle(sel, row_at, col_at, after(grads, token), *object_field.shape[1:])
        return mine_sum, other_sum

    def project(token, _):
        keep0, keep1, cross0, cross1 = updated
        return new_weights_of((after(keep0, token), keep1, cross0, cross1), stash)

    gram, (object_sums, new_weights) = sum_everywhere(gram, [put_back, project])
    new_object = object_field + OBJ_STEP * (object_sums[0] + swap_tiles(object_sums[1]))
    gram = after(gram, new_object)
    new_modes = new_modes_of(gram, summed, math.sqrt(pixels)).reshape(probe_modes.shape)
    return (new_object, new_modes, new_weights)


def solution(mesh):
    in_specs = (
        P(None, ("groups", "scan", "tile"), None),
        P(None, "groups", ("scan", "tile")),
        P(None, ("groups", "scan", "tile"), None),
        P(("groups", "scan", "tile"), None, None),
        P(("groups", "scan")),
        P(("groups", "scan")),
        P(("groups", "scan")),
        P(("groups", "scan")),
    )
    out_specs = (
        P(None, ("groups", "scan", "tile"), None),
        P(None, "groups", ("scan", "tile")),
        P(None, ("groups", "scan", "tile"), None),
    )
    return jax.shard_map(local, mesh=mesh, in_specs=in_specs, out_specs=out_specs, check_vma=False)
```

```python
import math

import jax
import jax.numpy as jnp
import numpy as np
from jax import lax
from jax.experimental import pallas as pl
from jax.experimental.pallas import tpu as pltpu
from jax.sharding import PartitionSpec as P

OBJ_STEP = 0.125
PROBE_STEP = 0.5
RB = 16
DEPTH = 3
f32 = jnp.float32
bf16 = jnp.bfloat16
HI = lax.Precision.HIGHEST


def transform_tables(length):
    ids = np.arange(length)
    angles = (ids[:, None] * ids[None, :] % length) * (2.0 * math.pi / length)
    cos_tab = np.cos(angles) / math.sqrt(length)
    sin_tab = np.sin(angles) / math.sqrt(length)
    forward = np.block([[cos_tab, sin_tab], [-sin_tab, cos_tab]])
    inverse = np.block([[cos_tab, -sin_tab], [sin_tab, cos_tab]])
    return jnp.asarray(forward, dtype=bf16), jnp.asarray(inverse, dtype=bf16)


def iota(shape, dim):
    return lax.broadcasted_iota(jnp.int32, shape, dim)


def widen_kernel(tab_ref, out_ref):
    rows, cols = tab_ref.shape[1:]
    tall, wide = out_ref.shape[1:]
    up = (iota((tall, rows), 0) // RB == iota((tall, rows), 1)).astype(bf16)
    across = (iota((cols, wide), 1) // RB == iota((cols, wide), 0)).astype(bf16)
    same = iota((tall, wide), 0) % RB == iota((tall, wide), 1) % RB
    for at in range(tab_ref.shape[0]):
        left = jnp.dot(up, tab_ref[at], preferred_element_type=f32).astype(bf16)
        full = jnp.dot(left, across, preferred_element_type=f32)
        out_ref[at] = jnp.where(same, full, 0.0).astype(bf16)


def widen(tables):
    count, rows, cols = tables.shape
    return pl.pallas_call(
        widen_kernel,
        out_shape=jax.ShapeDtypeStruct((count, rows * RB, cols * RB), bf16),
        compiler_params=pltpu.CompilerParams(vmem_limit_bytes=8 << 20),
        cost_estimate=pl.CostEstimate(flops=1 << 28, bytes_accessed=1 << 20, transcendentals=0),
        name="widen",
    )(tables)


def cut_kernel(meta_ref, owner_ref, row_ref, col_ref, obj_ref, out_ref):
    spot = pl.program_id(0) + meta_ref[0] * pl.num_programs(0)
    length = out_ref.shape[2]
    height, width = obj_ref.shape[2:]
    row_at, col_at = row_ref[spot], col_ref[spot]
    sel = (owner_ref[spot] != meta_ref[0]).astype(jnp.int32)
    rows = (iota((length, height), 1) == iota((length, height), 0) + row_at).astype(bf16)
    cols = (iota((width, length), 0) == iota((width, length), 1) + col_at).astype(bf16)
    for part in range(2):
        band = jnp.dot(rows, obj_ref[sel, part], preferred_element_type=f32).astype(bf16)
        out_ref[0, part] = jnp.dot(band, cols, preferred_element_type=f32).astype(bf16)


def cut_patches(obj_pair, scalars, cap, length):
    grid_spec = pltpu.PrefetchScalarGridSpec(
        num_scalar_prefetch=4,
        grid=(cap,),
        in_specs=[pl.BlockSpec(obj_pair.shape, lambda i, *_: (0, 0, 0, 0))],
        out_specs=pl.BlockSpec((1, 2, length, length), lambda i, *_: (i, 0, 0, 0)),
    )
    return pl.pallas_call(
        cut_kernel,
        grid_spec=grid_spec,
        out_shape=jax.ShapeDtypeStruct((cap, 2, length, length), bf16),
        compiler_params=pltpu.CompilerParams(vmem_limit_bytes=12 << 20),
        cost_estimate=pl.CostEstimate(flops=4 << 30, bytes_accessed=4 << 20, transcendentals=0),
        name="cut_patches",
    )(*scalars, obj_pair)


STEPS = (0, 2, 3, 1)


def place_of(meta_ref, j):
    count = len(STEPS)
    side, far_side, place = j // (2 * count), j // count % 2, j % count
    z, y, first = meta_ref[1], meta_ref[2], meta_ref[3]
    strip = 2 * ((z + STEPS[place]) % count) + (1 - y if far_side else y)
    return 2 * strip + (1 - first if side else first)


def relax_kernel(meta_ref, live_ref, mix_ref, *refs):
    count = len(STEPS)
    tab = [place_of(meta_ref, j) for j in range(4 * count)]
    blocks, refs = refs[:4 * count], refs[4 * count:]
    patch_ref, amp_ref, fwd_ref, inv_ref, keep0_ref, keep1_ref = refs[:6]
    cross0, cross1 = refs[6:6 + count], refs[6 + count:6 + 2 * count]
    grad_r_ref, grad_i_ref, stash_ref, probe_ref, new_ref, stash_sem = refs[6 + 2 * count:]
    group = pl.program_id(0)
    each = patch_ref.shape[0]
    length = patch_ref.shape[2]

    @pl.when(group == 0)
    def _():
        mix = mix_ref[0]
        for j, block_ref in enumerate(blocks):
            block = block_ref[...].reshape(block_ref.shape[0] * RB, length)
            mixed = jnp.dot(mix, block, preferred_element_type=f32)
            at = pl.multiple_of(tab[j] * RB, RB)
            probe_ref[:, pl.ds(at, RB), :] = mixed.reshape(mixed.shape[0] // RB, RB, length)

    def stashing(j):
        return pltpu.make_async_copy(blocks[j], stash_ref.at[j], stash_sem.at[j])

    @pl.when(group == 0)
    def _():
        for j in range(len(blocks)):
            stashing(j).start()

    def planes(q):
        spot = each * group + q
        return (probe_ref[2 * spot], probe_ref[2 * spot + 1],
                patch_ref[q, 0].astype(f32), patch_ref[q, 1].astype(f32))

    def leave(q):
        probe_r, probe_i, obj_r, obj_i = planes(q)
        exit_r = (probe_r * obj_r - probe_i * obj_i).astype(bf16)
        exit_i = (probe_r * obj_i + probe_i * obj_r).astype(bf16)
        return exit_r, exit_i

    def rows_pass(table, pairs):
        both = jnp.concatenate([jnp.concatenate(pair, axis=0) for pair in pairs], axis=1)
        out = jnp.dot(table[...], both, preferred_element_type=f32).astype(bf16)
        return jnp.concatenate([
            jnp.concatenate([out[:length, q * length:(q + 1) * length],
                             out[length:, q * length:(q + 1) * length]], axis=1)
            for q in range(each)], axis=0)

    def cols_pass(table, value):
        out = jnp.dot(value, table[...], preferred_element_type=f32)
        return [out[q * length:(q + 1) * length] for q in range(each)]

    def revise(q, far):
        far_r, far_i = far[:, :length], far[:, length:]
        scale = amp_ref[q].astype(f32) * lax.rsqrt(far_r * far_r + far_i * far_i + 1.0)
        return (far_r * scale).astype(bf16), (far_i * scale).astype(bf16)

    def update(q, exits, near):
        live = (each * group + q < live_ref[meta_ref[0]]).astype(f32)
        probe_r, probe_i, obj_r, obj_i = planes(q)
        delta_r = near[:, :length] - exits[0].astype(f32)
        delta_i = near[:, length:] - exits[1].astype(f32)
        grad_r_ref[q] = ((probe_r * delta_r + probe_i * delta_i) * live).astype(bf16)
        grad_i_ref[q] = ((probe_r * delta_i - probe_i * delta_r) * live).astype(bf16)
        change_r = obj_r * delta_r + obj_i * delta_i
        change_i = obj_r * delta_i - obj_i * delta_r
        for part, value in ((0, probe_r + PROBE_STEP * change_r), (1, probe_i + PROBE_STEP * change_i)):
            new_ref[2 * q + part] = (value * live).astype(bf16).reshape(4 * count, RB, length)

    exits = [leave(q) for q in range(each)]
    far = cols_pass(inv_ref, rows_pass(fwd_ref, exits))
    revised = [revise(q, far[q]) for q in range(each)]
    near = cols_pass(fwd_ref, rows_pass(inv_ref, revised))
    for q in range(each):
        update(q, exits[q], near[q])
    @pl.when(group == pl.num_programs(0) - 1)
    def _():
        for j in range(len(blocks)):
            stashing(j).wait()

    for j in range(4 * count):
        at = tab[j]
        side, far_side, place = j // (2 * count), j // count % 2, j % count
        for row in range(2 * each):
            if far_side:
                (cross1 if side else cross0)[place][row] = new_ref[row, at]
            else:
                (keep1_ref if side else keep0_ref)[place, row] = new_ref[row, at]


def whole(arr):
    return pl.BlockSpec(arr.shape, lambda *_: (0,) * arr.ndim)


def relax(meta, live, mix, blocks, patches, amplitude, forward, inverse):
    cap, _, length, _ = patches.shape
    count = len(STEPS)
    each = 4 if cap % 4 == 0 else 1
    plane = pl.BlockSpec((each, 2, length, length), lambda i, *_: (i, 0, 0, 0))
    strips = pl.BlockSpec((count, 2 * each, RB, length), lambda i, *_: (0, i, 0, 0))
    strip = pl.BlockSpec((2 * each, RB, length), lambda i, *_: (i, 0, 0))
    flat = pl.BlockSpec((each, length, length), lambda i, *_: (i, 0, 0))
    grid_spec = pltpu.PrefetchScalarGridSpec(
        num_scalar_prefetch=2,
        grid=(cap // each,),
        in_specs=[
            whole(mix), *[whole(block) for block in blocks], plane,
            flat,
            whole(forward), whole(inverse),
        ],
        out_specs=[strips, strips, *[strip] * (2 * count), flat, flat,
                   pl.BlockSpec(memory_space=pl.ANY)],
        scratch_shapes=[
            pltpu.VMEM((2 * cap, length, length), f32),
            pltpu.VMEM((2 * each, 4 * count, RB, length), bf16),
            pltpu.SemaphoreType.DMA((len(blocks),)),
        ],
    )
    many = jax.ShapeDtypeStruct((count, 2 * cap, RB, length), bf16)
    single = jax.ShapeDtypeStruct((2 * cap, RB, length), bf16)
    outs = pl.pallas_call(
        relax_kernel,
        grid_spec=grid_spec,
        out_shape=[many, many, *[single] * (2 * count),
                   pltpu.HBM((cap, length, length), bf16),
                   pltpu.HBM((cap, length, length), bf16),
                   pltpu.HBM((len(blocks),) + blocks[0].shape, bf16)],
        compiler_params=pltpu.CompilerParams(vmem_limit_bytes=28 << 20),
        cost_estimate=pl.CostEstimate(flops=8 << 30, bytes_accessed=16 << 20, transcendentals=1 << 19),
        name="relax_positions",
    )(meta, live, mix, *blocks, patches, amplitude, forward, inverse)
    return (outs[0], outs[1], outs[2:2 + count], outs[2 + count:2 + 2 * count]), outs[-3:-1], outs[-1]


def settle_kernel(meta_ref, owner_ref, row_ref, col_ref, grad_ref, mine_ref, other_ref, band_ref):
    cap, length, _ = grad_ref.shape
    height, width = mine_ref.shape
    places = []
    for spot in range(cap):
        at = spot + meta_ref[0] * cap
        row_at, col_at = row_ref[at], col_ref[at]
        sel = (owner_ref[at] != meta_ref[0]).astype(jnp.int32)
        cols = (iota((length, width), 1) == iota((length, width), 0) + col_at).astype(bf16)
        band = jnp.dot(grad_ref[spot], cols, preferred_element_type=f32)
        band_ref[spot * length:(spot + 1) * length] = band.astype(bf16)
        place = iota((2 * height, length), 1) + row_at + height * sel
        places.append((iota((2 * height, length), 0) == place).astype(bf16))
    places = jnp.concatenate(places, axis=1)
    total = jnp.dot(places, band_ref[...], preferred_element_type=f32)
    mine_ref[...] = total[:height]
    other_ref[...] = total[height:]


def settle(scalars, grads, height, width):
    cap, length, _ = grads.shape
    tile = pl.BlockSpec((height, width), lambda *_: (0, 0))
    grid_spec = pltpu.PrefetchScalarGridSpec(
        num_scalar_prefetch=4,
        grid=(1,),
        in_specs=[whole(grads)],
        out_specs=[tile, tile],
        scratch_shapes=[pltpu.VMEM((cap * length, width), bf16)],
    )
    shape = jax.ShapeDtypeStruct((height, width), f32)
    return pl.pallas_call(
        settle_kernel,
        grid_spec=grid_spec,
        out_shape=[shape, shape],
        compiler_params=pltpu.CompilerParams(vmem_limit_bytes=20 << 20),
        cost_estimate=pl.CostEstimate(flops=2 << 30, bytes_accessed=4 << 20, transcendentals=0),
        name="settle",
    )(*scalars, grads)


def weights_kernel(keep0_ref, keep1_ref, *refs):
    count = len(STEPS)
    cross, (block_ref, nw_ref) = refs[:2 * count], refs[2 * count:]
    lanes = keep0_ref.shape[3]
    tall = keep0_ref.shape[1] * RB
    wide = block_ref.shape[1] * RB
    table = jnp.zeros((tall, wide), f32)
    for j in range(4 * count):
        side, far_side, place = j // (2 * count), j // count % 2, j % count
        if far_side:
            mine = cross[count * side + place][...]
        else:
            mine = (keep1_ref if side else keep0_ref)[place]
        table += lax.dot_general(mine.reshape(tall, lanes), block_ref[j].reshape(wide, lanes),
                                 (((1,), (1,)), ((), ())), preferred_element_type=f32)
    same = (iota((tall, wide), 0) % RB) == (iota((tall, wide), 1) % RB)
    table = jnp.where(same, table, 0.0)
    slots, modes = tall // (2 * RB), wide // (2 * RB)

    def mul(left, right):
        return jnp.dot(left, right, precision=HI, preferred_element_type=f32)

    def gather_rows(which):
        pick = iota((slots, tall), 1) // RB == 2 * iota((slots, tall), 0) + which
        return mul(pick.astype(f32), table)

    def pick_cols(which):
        pick = iota((wide, modes), 0) // RB == which * modes + iota((wide, modes), 1)
        return pick.astype(f32)

    low, high = gather_rows(0), gather_rows(1)
    cols_r, cols_i = pick_cols(0), pick_cols(1)
    norm = 1.0 / (4 * count * RB * lanes)
    nw_ref[0] = (mul(low, cols_r) + mul(high, cols_i)) * norm
    nw_ref[1] = (mul(high, cols_r) - mul(low, cols_i)) * norm


def new_weights_of(updated, blocks):
    keep0, keep1, cross0, cross1 = updated
    args = [keep0, keep1, *cross0, *cross1, blocks]
    return pl.pallas_call(
        weights_kernel,
        out_shape=jax.ShapeDtypeStruct((2, keep0.shape[1] // 2, blocks.shape[1] // 2), f32),
        compiler_params=pltpu.CompilerParams(vmem_limit_bytes=16 << 20),
        cost_estimate=pl.CostEstimate(flops=2 << 30, bytes_accessed=6 << 20, transcendentals=0),
        name="new_weights",
    )(*args)


def sums_kernel(wide_ref, near_ref, twin_ref, far_ref, far_twin_ref, out_ref):
    lanes = near_ref.shape[-1]

    def flat(value):
        return value.reshape(-1, lanes)

    total = jnp.dot(wide_ref[0], flat(near_ref[0]), preferred_element_type=f32)
    total += jnp.dot(wide_ref[1], flat(twin_ref[0]), preferred_element_type=f32)
    total += jnp.dot(wide_ref[2], flat(far_ref[...]), preferred_element_type=f32)
    total += jnp.dot(wide_ref[3], flat(far_twin_ref[...]), preferred_element_type=f32)
    out_ref[...] = total.reshape(out_ref.shape).astype(out_ref.dtype)


def pair_sums(place, wide, near, twin, far, far_twin, kind):
    lanes = near.shape[-1]
    strip = pl.BlockSpec((1,) + near.shape[1:], lambda i: (place, 0, 0, 0))
    tall = wide.shape[1] // RB
    return pl.pallas_call(
        sums_kernel,
        grid=(1,),
        in_specs=[whole(wide), strip, strip, whole(far), whole(far_twin)],
        out_specs=pl.BlockSpec((tall, RB, lanes), lambda *_: (0, 0, 0)),
        out_shape=jax.ShapeDtypeStruct((tall, RB, lanes), kind),
        compiler_params=pltpu.CompilerParams(vmem_limit_bytes=8 << 20),
        cost_estimate=pl.CostEstimate(flops=1 << 29, bytes_accessed=2 << 20, transcendentals=0),
        name="mode_sums",
    )(wide, near, twin, far, far_twin)


def finish_kernel(*refs):
    own_ref, others = refs[0], refs[1:-3]
    sum_ref, gram_ref, acc_ref = refs[-3:]
    lanes = own_ref.shape[-1]
    total = own_ref[...]
    for other in others:
        total = total + other[...].astype(f32)
    acc_ref[...] = total
    for row in range(RB):
        sum_ref[:, row * lanes:(row + 1) * lanes] = acc_ref[:, row, :]
    modes = sum_ref.shape[0] // 2
    flat = sum_ref[...]
    full = lax.dot_general(flat, flat, (((1,), (1,)), ((), ())), precision=HI,
                           preferred_element_type=f32)
    gram_ref[0] = full[:modes, :modes] + full[modes:, modes:]
    gram_ref[1] = full[modes:, :modes] - full[:modes, modes:]


def finish_sums(own, others):
    tall, _, lanes = own.shape
    return pl.pallas_call(
        finish_kernel,
        out_shape=[
            jax.ShapeDtypeStruct((tall, RB * lanes), f32),
            jax.ShapeDtypeStruct((2, tall // 2, tall // 2), f32),
        ],
        scratch_shapes=[pltpu.VMEM((tall, RB, lanes), f32)],
        compiler_params=pltpu.CompilerParams(vmem_limit_bytes=8 << 20),
        cost_estimate=pl.CostEstimate(flops=1 << 28, bytes_accessed=2 << 20, transcendentals=0),
        name="finish_sums",
    )(own, *others)


def modes_kernel(norm, gram_ref, sum_ref, out_ref):
    count = gram_ref.shape[1]
    gram_r, gram_i = gram_ref[0], gram_ref[1]
    eye = (iota((count, count), 0) == iota((count, count), 1)).astype(f32)
    zero = jnp.zeros((count, count), f32)
    work = jnp.concatenate([gram_r, gram_i, eye, zero], axis=1)
    turned = jnp.concatenate([-gram_i, gram_r, zero, eye], axis=1)
    row_ids = iota((count, 1), 0)
    roots = jnp.zeros((count, 1), f32)
    for pivot in range(count):
        lead = work[pivot:pivot + 1, pivot:pivot + 1]
        roots = jnp.where(row_ids == pivot, lead, roots)
        if pivot + 1 < count:
            below = jnp.where(row_ids > pivot, 1.0 / lead, 0.0)
            coef_r = work[:, pivot:pivot + 1] * below
            coef_i = work[:, count + pivot:count + pivot + 1] * below
            row, row_t = work[pivot:pivot + 1], turned[pivot:pivot + 1]
            work = work - (coef_r * row + coef_i * row_t)
            turned = turned - (coef_r * row_t - coef_i * row)
    back = work[:, 2 * count:] * (norm * lax.rsqrt(roots))
    back_r, back_i = back[:, :count], back[:, count:]
    full = jnp.concatenate([
        jnp.concatenate([back_r, -back_i], axis=1),
        jnp.concatenate([back_i, back_r], axis=1)], axis=0)
    full_top = full.astype(bf16)
    full_rest = (full - full_top.astype(f32)).astype(bf16)
    flat = sum_ref[...]
    flat_top = flat.astype(bf16)
    flat_rest = (flat - flat_top.astype(f32)).astype(bf16)
    left = jnp.concatenate([full_top, full_top, full_rest], axis=1)
    right = jnp.concatenate([flat_top, flat_rest, flat_top], axis=0)
    out_ref[...] = jnp.dot(left, right, preferred_element_type=f32)


def new_modes_of(gram, summed, norm):
    def kernel(gram_ref, sum_ref, out_ref):
        modes_kernel(norm, gram_ref, sum_ref, out_ref)

    return pl.pallas_call(
        kernel,
        out_shape=jax.ShapeDtypeStruct(summed.shape, f32),
        compiler_params=pltpu.CompilerParams(vmem_limit_bytes=8 << 20),
        cost_estimate=pl.CostEstimate(flops=1 << 27, bytes_accessed=1 << 20, transcendentals=256),
        name="orthonormal_modes",
    )(gram, summed)


def swap_tiles(value):
    count = lax.axis_size("tile")
    return lax.ppermute(value, "tile", [(i, (i + 1) % count) for i in range(count)])


def turn(value, step):
    count = lax.axis_size("scan")
    return lax.ppermute(value, "scan", [(i, (i + 2 * step) % count) for i in range(count)])


def across(value):
    count = lax.axis_size("scan")
    return lax.ppermute(value, "scan", [(i, i ^ 1) for i in range(count)])


def after(value, *others):
    return lax.optimization_barrier((value, *others))[0]


def gather_blocks(own, obj_b, cut, ready):
    come = {1: turn(own, 1), 3: turn(own, 3)}
    side = {0: across(own)}
    obj_pair = jnp.stack([obj_b, swap_tiles(obj_b)])
    patches = cut(obj_pair)
    patches, come[1], come[3], ready = lax.optimization_barrier((patches, come[1], come[3], ready))
    come[2] = turn(come[1], 1)
    for step in (1, 3, 2):
        side[step] = across(come[step])
    come[0] = own
    order = [-step % len(STEPS) for step in STEPS]
    mine = [come[step] for step in order] + [side[step] for step in order]
    return mine + [swap_tiles(value) for value in mine], patches, ready


def gather_any(own, obj_b, cut, ready):
    rows = own.shape[1]
    every = lax.all_gather(own, ("scan", "tile"))
    every = every.reshape((-1, RB // rows) + own.shape).transpose(0, 2, 1, 3, 4)
    every = every.reshape(-1, own.shape[0], RB, own.shape[2])
    blocks = [every[4 * step + 2 * y + tile] for tile in (0, 1) for y in (0, 1) for step in STEPS]
    return blocks, cut(jnp.stack([obj_b, swap_tiles(obj_b)])), ready


def gather_mixing(weights_b):
    wt_r, wt_i = jnp.swapaxes(weights_b[0], 0, 1), jnp.swapaxes(weights_b[1], 0, 1)
    real_rows = jnp.stack([wt_r, wt_i], axis=2)
    imag_rows = jnp.stack([-wt_i, wt_r], axis=2)
    count, cap = wt_r.shape
    return jnp.stack([real_rows, imag_rows], axis=0).reshape(2 * count, 2 * cap)


def scatter_sums(weights_b, updated, blocks):
    keep0, keep1, cross0, cross1 = updated
    pair = jnp.stack([weights_b, swap_tiles(weights_b)])
    pair = after(pair, blocks[-1])
    quad = jnp.concatenate([pair, across(pair)])
    wide = widen(jax.vmap(gather_mixing)(quad))
    order = (2, 3, 1, 0)
    at = {step: STEPS.index(step) for step in order}
    twin_cross = {step: swap_tiles(cross1[at[step]]) for step in order}
    twin = swap_tiles(keep1)
    far, far_twin, line = {}, {}, []
    for step in order:
        for value, dest in ((cross0[at[step]], far), (twin_cross[step], far_twin)):
            dest[step] = across(after(value, line[-DEPTH]) if len(line) >= DEPTH else value)
            line.append(dest[step])
    def part(step, kind):
        return pair_sums(at[step], wide, keep0, twin, far[step], far_twin[step], kind)

    through = turn(part(2, bf16), 1)
    third = turn(part(3, bf16), 3)
    first = turn((part(1, f32) + through.astype(f32)).astype(bf16), 1)
    return finish_sums(part(0, f32), [first, third])


def scatter_any(weights_b, updated, _):
    devices = lax.axis_size("scan") * lax.axis_size("tile")
    keep0, keep1, cross0, cross1 = updated
    count, slots, _, length = keep0.shape
    every = lax.all_gather(weights_b, ("scan", "tile"))
    rows = 4 * count * RB // devices
    parts = jnp.stack([keep0, keep1, jnp.stack(cross0), jnp.stack(cross1)], axis=1)
    parts = jnp.stack([parts[STEPS.index(step)] for step in range(count)])
    parts = parts.reshape(4 * count, slots, RB // rows, rows, length)
    parts = parts.transpose(0, 2, 1, 3, 4).reshape(devices, slots, rows, length)
    arrived = lax.all_to_all(parts, ("scan", "tile"), split_axis=0, concat_axis=0, tiled=True)
    flat = arrived.reshape(devices, slots // 2, 2, rows * length).astype(f32)
    wt_r, wt_i = every[:, 0].astype(f32), every[:, 1].astype(f32)
    up_r, up_i = flat[:, :, 0], flat[:, :, 1]

    def mul(left, right):
        return jnp.einsum("dpk,dpx->kx", left, right, precision=HI)

    sum_r = mul(wt_r, up_r) + mul(wt_i, up_i)
    sum_i = mul(wt_r, up_i) - mul(wt_i, up_r)

    def pair(left, right):
        return jnp.dot(left, right.T, precision=HI)

    gram = jnp.stack([pair(sum_r, sum_r) + pair(sum_i, sum_i),
                      pair(sum_i, sum_r) - pair(sum_r, sum_i)])
    return jnp.concatenate([sum_r, sum_i]), gram


def sum_everywhere(value, works):
    value = value + swap_tiles(value)
    count = lax.axis_size("scan")
    step, works = 1, list(works)
    results = []
    while step < count:
        come = lax.ppermute(value, "scan", [(i, i ^ step) for i in range(count)])
        step *= 2
        if works:
            value, come, result = lax.optimization_barrier((value, come, works.pop(0)(value)))
            results.append(result)
        value = value + come
    return value, results


def local(
    object_field, probe_modes, weights, amplitude, slot_count, tile_owner, corner_row, corner_col
):
    n_tile = lax.axis_size("tile")
    devices = lax.axis_size("scan") * n_tile
    tile = lax.axis_index("tile")
    cap, length, _ = amplitude.shape
    count = probe_modes.shape[1]
    pixels = length * length
    rows = length // devices
    forward, inverse = transform_tables(length)

    own = probe_modes.astype(bf16).reshape(2 * count, rows, length)
    obj_b = object_field.astype(bf16)
    weights_b = weights.astype(bf16)
    planned = lax.axis_size("scan") == 8 and n_tile == 2 and rows == RB

    scan = lax.axis_index("scan")
    zero = jnp.zeros_like(scan)
    meta = jnp.stack([tile, scan // 2, scan % 2, tile] if planned else [tile, zero, zero, zero])
    meta = meta.astype(jnp.int32)
    scalars = (meta, tile_owner, corner_row, corner_col)

    def cut(obj_pair):
        return cut_patches(obj_pair, scalars, cap, length)

    wt_r, wt_i = weights_b[0], weights_b[1]
    mix = jnp.stack([jnp.concatenate([wt_r, -wt_i], axis=1),
                     jnp.concatenate([wt_i, wt_r], axis=1)], axis=1)
    mix = widen(mix.reshape(1, 2 * cap, 2 * count))
    blocks, patches, (mix, forward, inverse) = (gather_blocks if planned else gather_any)(
        own, obj_b, cut, (mix, forward, inverse))
    updated, grads, stash = relax(meta, slot_count, mix, blocks, patches, amplitude, forward, inverse)

    def put_back(part):
        return lambda token: settle(scalars, after(grads[part], token), *object_field.shape[1:])

    summed, gram = (scatter_sums if planned else scatter_any)(weights_b, updated, blocks)

    def project(token):
        keep0, keep1, cross0, cross1 = updated
        return new_weights_of((after(keep0, token), keep1, cross0, cross1), stash)

    gram, (real, imag, new_weights) = sum_everywhere(gram, [put_back(0), put_back(1), project])
    steps = [mine_sum + swap_tiles(other_sum) for mine_sum, other_sum in (real, imag)]
    new_object = object_field + OBJ_STEP * jnp.stack(steps)
    new_modes = new_modes_of(gram, summed, math.sqrt(pixels)).reshape(probe_modes.shape)
    return (new_object, new_modes, new_weights)


def solution(mesh):
    in_specs = (
        P(None, ("groups", "scan", "tile"), None),
        P(None, "groups", ("scan", "tile")),
        P(None, ("groups", "scan", "tile"), None),
        P(("groups", "scan", "tile"), None, None),
        P(("groups", "scan")),
        P(("groups", "scan")),
        P(("groups", "scan")),
        P(("groups", "scan")),
    )
    out_specs = (
        P(None, ("groups", "scan", "tile"), None),
        P(None, "groups", ("scan", "tile")),
        P(None, ("groups", "scan", "tile"), None),
    )
    return jax.shard_map(local, mesh=mesh, in_specs=in_specs, out_specs=out_specs, check_vma=False)
```

```python
import math

import jax
import jax.numpy as jnp
import numpy as np
from jax import lax
from jax.experimental import pallas as pl
from jax.experimental.pallas import tpu as pltpu
from jax.sharding import PartitionSpec as P

OBJ_STEP = 0.125
PROBE_STEP = 0.5
RB = 16
DEPTH = 3
f32 = jnp.float32
bf16 = jnp.bfloat16
HI = lax.Precision.HIGHEST


def transform_tables(length):
    ids = np.arange(length)
    angles = (ids[:, None] * ids[None, :] % length) * (2.0 * math.pi / length)
    cos_tab = np.cos(angles) / math.sqrt(length)
    sin_tab = np.sin(angles) / math.sqrt(length)
    forward = np.block([[cos_tab, sin_tab], [-sin_tab, cos_tab]])
    inverse = np.block([[cos_tab, -sin_tab], [sin_tab, cos_tab]])
    return jnp.asarray(forward, dtype=bf16), jnp.asarray(inverse, dtype=bf16)


def iota(shape, dim):
    return lax.broadcasted_iota(jnp.int32, shape, dim)


def widen_kernel(tab_ref, out_ref):
    rows, cols = tab_ref.shape[1:]
    tall, wide = out_ref.shape[1:]
    up = (iota((tall, rows), 0) // RB == iota((tall, rows), 1)).astype(bf16)
    across = (iota((cols, wide), 1) // RB == iota((cols, wide), 0)).astype(bf16)
    same = iota((tall, wide), 0) % RB == iota((tall, wide), 1) % RB
    for at in range(tab_ref.shape[0]):
        left = jnp.dot(up, tab_ref[at], preferred_element_type=f32).astype(bf16)
        full = jnp.dot(left, across, preferred_element_type=f32)
        out_ref[at] = jnp.where(same, full, 0.0).astype(bf16)


def widen(tables):
    count, rows, cols = tables.shape
    return pl.pallas_call(
        widen_kernel,
        out_shape=jax.ShapeDtypeStruct((count, rows * RB, cols * RB), bf16),
        compiler_params=pltpu.CompilerParams(vmem_limit_bytes=8 << 20),
        cost_estimate=pl.CostEstimate(flops=1 << 28, bytes_accessed=1 << 20, transcendentals=0),
        name="widen",
    )(tables)


def cut_kernel(meta_ref, owner_ref, row_ref, col_ref, obj_ref, out_ref):
    spot = pl.program_id(0) + meta_ref[0] * pl.num_programs(0)
    length = out_ref.shape[2]
    height, width = obj_ref.shape[2:]
    row_at, col_at = row_ref[spot], col_ref[spot]
    sel = (owner_ref[spot] != meta_ref[0]).astype(jnp.int32)
    rows = (iota((length, height), 1) == iota((length, height), 0) + row_at).astype(bf16)
    cols = (iota((width, length), 0) == iota((width, length), 1) + col_at).astype(bf16)
    for part in range(2):
        band = jnp.dot(rows, obj_ref[sel, part], preferred_element_type=f32).astype(bf16)
        out_ref[0, part] = jnp.dot(band, cols, preferred_element_type=f32).astype(bf16)


def cut_patches(obj_pair, scalars, cap, length):
    grid_spec = pltpu.PrefetchScalarGridSpec(
        num_scalar_prefetch=4,
        grid=(cap,),
        in_specs=[pl.BlockSpec(obj_pair.shape, lambda i, *_: (0, 0, 0, 0))],
        out_specs=pl.BlockSpec((1, 2, length, length), lambda i, *_: (i, 0, 0, 0)),
    )
    return pl.pallas_call(
        cut_kernel,
        grid_spec=grid_spec,
        out_shape=jax.ShapeDtypeStruct((cap, 2, length, length), bf16),
        compiler_params=pltpu.CompilerParams(vmem_limit_bytes=12 << 20),
        cost_estimate=pl.CostEstimate(flops=4 << 30, bytes_accessed=4 << 20, transcendentals=0),
        name="cut_patches",
    )(*scalars, obj_pair)


STEPS = (0, 2, 3, 1)


def place_of(meta_ref, j):
    count = len(STEPS)
    side, far_side, place = j // (2 * count), j // count % 2, j % count
    z, y, first = meta_ref[1], meta_ref[2], meta_ref[3]
    strip = 2 * ((z + STEPS[place]) % count) + (1 - y if far_side else y)
    return 2 * strip + (1 - first if side else first)


def relax_kernel(meta_ref, live_ref, mix_ref, *refs):
    count = len(STEPS)
    tab = [place_of(meta_ref, j) for j in range(4 * count)]
    blocks, refs = refs[:4 * count], refs[4 * count:]
    patch_ref, amp_ref, fwd_ref, inv_ref, keep0_ref, keep1_ref = refs[:6]
    cross0, cross1 = refs[6:6 + count], refs[6 + count:6 + 2 * count]
    grad_r_ref, grad_i_ref, stash_ref, probe_ref, new_ref, stash_sem = refs[6 + 2 * count:]
    group = pl.program_id(0)
    each = patch_ref.shape[0]
    length = patch_ref.shape[2]

    @pl.when(group == 0)
    def _():
        mix = mix_ref[0]
        for j, block_ref in enumerate(blocks):
            block = block_ref[...].reshape(block_ref.shape[0] * RB, length)
            mixed = jnp.dot(mix, block, preferred_element_type=f32)
            at = pl.multiple_of(tab[j] * RB, RB)
            probe_ref[:, pl.ds(at, RB), :] = mixed.reshape(mixed.shape[0] // RB, RB, length)

    def stashing(j):
        return pltpu.make_async_copy(blocks[j], stash_ref.at[j], stash_sem.at[j])

    @pl.when(group == 0)
    def _():
        for j in range(len(blocks)):
            stashing(j).start()

    def planes(q):
        spot = each * group + q
        return (probe_ref[2 * spot], probe_ref[2 * spot + 1],
                patch_ref[q, 0].astype(f32), patch_ref[q, 1].astype(f32))

    def leave(q):
        probe_r, probe_i, obj_r, obj_i = planes(q)
        exit_r = (probe_r * obj_r - probe_i * obj_i).astype(bf16)
        exit_i = (probe_r * obj_i + probe_i * obj_r).astype(bf16)
        return exit_r, exit_i

    def rows_pass(table, pairs):
        both = jnp.concatenate([jnp.concatenate(pair, axis=0) for pair in pairs], axis=1)
        out = jnp.dot(table[...], both, preferred_element_type=f32).astype(bf16)
        return jnp.concatenate([
            jnp.concatenate([out[:length, q * length:(q + 1) * length],
                             out[length:, q * length:(q + 1) * length]], axis=1)
            for q in range(each)], axis=0)

    def cols_pass(table, value):
        out = jnp.dot(value, table[...], preferred_element_type=f32)
        return [out[q * length:(q + 1) * length] for q in range(each)]

    def revise(q, far):
        far_r, far_i = far[:, :length], far[:, length:]
        scale = amp_ref[q].astype(f32) * lax.rsqrt(far_r * far_r + far_i * far_i + 1.0)
        return (far_r * scale).astype(bf16), (far_i * scale).astype(bf16)

    def update(q, exits, near):
        live = (each * group + q < live_ref[meta_ref[0]]).astype(f32)
        probe_r, probe_i, obj_r, obj_i = planes(q)
        delta_r = near[:, :length] - exits[0].astype(f32)
        delta_i = near[:, length:] - exits[1].astype(f32)
        grad_r_ref[q] = ((probe_r * delta_r + probe_i * delta_i) * live).astype(bf16)
        grad_i_ref[q] = ((probe_r * delta_i - probe_i * delta_r) * live).astype(bf16)
        change_r = obj_r * delta_r + obj_i * delta_i
        change_i = obj_r * delta_i - obj_i * delta_r
        for part, value in ((0, probe_r + PROBE_STEP * change_r), (1, probe_i + PROBE_STEP * change_i)):
            new_ref[2 * q + part] = (value * live).astype(bf16).reshape(4 * count, RB, length)

    exits = [leave(q) for q in range(each)]
    far = cols_pass(inv_ref, rows_pass(fwd_ref, exits))
    revised = [revise(q, far[q]) for q in range(each)]
    near = cols_pass(fwd_ref, rows_pass(inv_ref, revised))
    for q in range(each):
        update(q, exits[q], near[q])
    @pl.when(group == pl.num_programs(0) - 1)
    def _():
        for j in range(len(blocks)):
            stashing(j).wait()

    for j in range(4 * count):
        at = tab[j]
        side, far_side, place = j // (2 * count), j // count % 2, j % count
        for row in range(2 * each):
            if far_side:
                (cross1 if side else cross0)[place][row] = new_ref[row, at]
            else:
                (keep1_ref if side else keep0_ref)[place, row] = new_ref[row, at]


def whole(arr):
    return pl.BlockSpec(arr.shape, lambda *_: (0,) * arr.ndim)


def relax(meta, live, mix, blocks, patches, amplitude, forward, inverse):
    cap, _, length, _ = patches.shape
    count = len(STEPS)
    each = 4 if cap % 4 == 0 else 1
    plane = pl.BlockSpec((each, 2, length, length), lambda i, *_: (i, 0, 0, 0))
    strips = pl.BlockSpec((count, 2 * each, RB, length), lambda i, *_: (0, i, 0, 0))
    strip = pl.BlockSpec((2 * each, RB, length), lambda i, *_: (i, 0, 0))
    flat = pl.BlockSpec((each, length, length), lambda i, *_: (i, 0, 0))
    grid_spec = pltpu.PrefetchScalarGridSpec(
        num_scalar_prefetch=2,
        grid=(cap // each,),
        in_specs=[
            whole(mix), *[whole(block) for block in blocks], plane,
            flat,
            whole(forward), whole(inverse),
        ],
        out_specs=[strips, strips, *[strip] * (2 * count), flat, flat,
                   pl.BlockSpec(memory_space=pl.ANY)],
        scratch_shapes=[
            pltpu.VMEM((2 * cap, length, length), f32),
            pltpu.VMEM((2 * each, 4 * count, RB, length), bf16),
            pltpu.SemaphoreType.DMA((len(blocks),)),
        ],
    )
    many = jax.ShapeDtypeStruct((count, 2 * cap, RB, length), bf16)
    single = jax.ShapeDtypeStruct((2 * cap, RB, length), bf16)
    outs = pl.pallas_call(
        relax_kernel,
        grid_spec=grid_spec,
        out_shape=[many, many, *[single] * (2 * count),
                   pltpu.HBM((cap, length, length), bf16),
                   pltpu.HBM((cap, length, length), bf16),
                   pltpu.HBM((len(blocks),) + blocks[0].shape, bf16)],
        compiler_params=pltpu.CompilerParams(vmem_limit_bytes=28 << 20),
        cost_estimate=pl.CostEstimate(flops=8 << 30, bytes_accessed=16 << 20, transcendentals=1 << 19),
        name="relax_positions",
    )(meta, live, mix, *blocks, patches, amplitude, forward, inverse)
    return (outs[0], outs[1], outs[2:2 + count], outs[2 + count:2 + 2 * count]), outs[-3:-1], outs[-1]


def settle_kernel(meta_ref, owner_ref, row_ref, col_ref, grad_ref, mine_ref, other_ref, band_ref):
    cap, length, _ = grad_ref.shape
    height, width = mine_ref.shape
    places = []
    for spot in range(cap):
        at = spot + meta_ref[0] * cap
        row_at, col_at = row_ref[at], col_ref[at]
        sel = (owner_ref[at] != meta_ref[0]).astype(jnp.int32)
        cols = (iota((length, width), 1) == iota((length, width), 0) + col_at).astype(bf16)
        band = jnp.dot(grad_ref[spot], cols, preferred_element_type=f32).astype(bf16)
        for which in range(2):
            flag = (sel == which).astype(f32).astype(bf16)
            band_ref[spot * length:(spot + 1) * length, which * width:(which + 1) * width] = band * flag
        places.append((iota((height, length), 0) == iota((height, length), 1) + row_at).astype(bf16))
    places = jnp.concatenate(places, axis=1)
    total = jnp.dot(places, band_ref[...], preferred_element_type=f32)
    mine_ref[...] = total[:, :width]
    other_ref[...] = total[:, width:]


def settle(scalars, grads, height, width):
    cap, length, _ = grads.shape
    tile = pl.BlockSpec((height, width), lambda *_: (0, 0))
    grid_spec = pltpu.PrefetchScalarGridSpec(
        num_scalar_prefetch=4,
        grid=(1,),
        in_specs=[whole(grads)],
        out_specs=[tile, tile],
        scratch_shapes=[pltpu.VMEM((cap * length, 2 * width), bf16)],
    )
    shape = jax.ShapeDtypeStruct((height, width), f32)
    return pl.pallas_call(
        settle_kernel,
        grid_spec=grid_spec,
        out_shape=[shape, shape],
        compiler_params=pltpu.CompilerParams(vmem_limit_bytes=20 << 20),
        cost_estimate=pl.CostEstimate(flops=2 << 30, bytes_accessed=4 << 20, transcendentals=0),
        name="settle",
    )(*scalars, grads)


def weights_kernel(keep0_ref, keep1_ref, *refs):
    count = len(STEPS)
    cross, (block_ref, nw_ref) = refs[:2 * count], refs[2 * count:]
    lanes = keep0_ref.shape[3]
    tall = keep0_ref.shape[1] * RB
    wide = block_ref.shape[1] * RB
    table = jnp.zeros((tall, wide), f32)
    for j in range(4 * count):
        side, far_side, place = j // (2 * count), j // count % 2, j % count
        if far_side:
            mine = cross[count * side + place][...]
        else:
            mine = (keep1_ref if side else keep0_ref)[place]
        table += lax.dot_general(mine.reshape(tall, lanes), block_ref[j].reshape(wide, lanes),
                                 (((1,), (1,)), ((), ())), preferred_element_type=f32)
    same = (iota((tall, wide), 0) % RB) == (iota((tall, wide), 1) % RB)
    table = jnp.where(same, table, 0.0)
    slots, modes = tall // (2 * RB), wide // (2 * RB)

    def mul(left, right):
        return jnp.dot(left, right, precision=HI, preferred_element_type=f32)

    rows = jnp.sum(table.reshape(2 * slots, RB, wide), axis=1)
    pick = (iota((wide, 2 * modes), 0) // RB == iota((wide, 2 * modes), 1)).astype(f32)
    small = mul(rows, pick)

    def every_other(which):
        return mul((iota((slots, 2 * slots), 1) == 2 * iota((slots, 2 * slots), 0) + which).astype(f32), small)

    low, high = every_other(0), every_other(1)
    norm = 1.0 / (4 * count * RB * lanes)
    nw_ref[0] = (low[:, :modes] + high[:, modes:]) * norm
    nw_ref[1] = (high[:, :modes] - low[:, modes:]) * norm


def new_weights_of(updated, blocks):
    keep0, keep1, cross0, cross1 = updated
    args = [keep0, keep1, *cross0, *cross1, blocks]
    return pl.pallas_call(
        weights_kernel,
        out_shape=jax.ShapeDtypeStruct((2, keep0.shape[1] // 2, blocks.shape[1] // 2), f32),
        compiler_params=pltpu.CompilerParams(vmem_limit_bytes=16 << 20),
        cost_estimate=pl.CostEstimate(flops=2 << 30, bytes_accessed=6 << 20, transcendentals=0),
        name="new_weights",
    )(*args)


def sums_kernel(wide_ref, near_ref, twin_ref, far_ref, far_twin_ref, out_ref):
    lanes = near_ref.shape[-1]

    def flat(value):
        return value.reshape(-1, lanes)

    total = jnp.dot(wide_ref[0], flat(near_ref[0]), preferred_element_type=f32)
    total += jnp.dot(wide_ref[1], flat(twin_ref[0]), preferred_element_type=f32)
    total += jnp.dot(wide_ref[2], flat(far_ref[...]), preferred_element_type=f32)
    total += jnp.dot(wide_ref[3], flat(far_twin_ref[...]), preferred_element_type=f32)
    out_ref[...] = total.reshape(out_ref.shape).astype(out_ref.dtype)


def pair_sums(place, wide, near, twin, far, far_twin, kind):
    lanes = near.shape[-1]
    strip = pl.BlockSpec((1,) + near.shape[1:], lambda i: (place, 0, 0, 0))
    tall = wide.shape[1] // RB
    return pl.pallas_call(
        sums_kernel,
        grid=(1,),
        in_specs=[whole(wide), strip, strip, whole(far), whole(far_twin)],
        out_specs=pl.BlockSpec((tall, RB, lanes), lambda *_: (0, 0, 0)),
        out_shape=jax.ShapeDtypeStruct((tall, RB, lanes), kind),
        compiler_params=pltpu.CompilerParams(vmem_limit_bytes=8 << 20),
        cost_estimate=pl.CostEstimate(flops=1 << 29, bytes_accessed=2 << 20, transcendentals=0),
        name="mode_sums",
    )(wide, near, twin, far, far_twin)


def finish_kernel(*refs):
    own_ref, others = refs[0], refs[1:-3]
    sum_ref, gram_ref, acc_ref = refs[-3:]
    lanes = own_ref.shape[-1]
    total = own_ref[...]
    for other in others:
        total = total + other[...].astype(f32)
    acc_ref[...] = total
    for row in range(RB):
        sum_ref[:, row * lanes:(row + 1) * lanes] = acc_ref[:, row, :]
    modes = sum_ref.shape[0] // 2
    flat = sum_ref[...]
    full = lax.dot_general(flat, flat, (((1,), (1,)), ((), ())), precision=HI,
                           preferred_element_type=f32)
    gram_ref[0] = full[:modes, :modes] + full[modes:, modes:]
    gram_ref[1] = full[modes:, :modes] - full[:modes, modes:]


def finish_sums(own, others):
    tall, _, lanes = own.shape
    return pl.pallas_call(
        finish_kernel,
        out_shape=[
            jax.ShapeDtypeStruct((tall, RB * lanes), f32),
            jax.ShapeDtypeStruct((2, tall // 2, tall // 2), f32),
        ],
        scratch_shapes=[pltpu.VMEM((tall, RB, lanes), f32)],
        compiler_params=pltpu.CompilerParams(vmem_limit_bytes=8 << 20),
        cost_estimate=pl.CostEstimate(flops=1 << 28, bytes_accessed=2 << 20, transcendentals=0),
        name="finish_sums",
    )(own, *others)


def modes_kernel(norm, gram_ref, sum_ref, out_ref):
    count = gram_ref.shape[1]
    gram_r, gram_i = gram_ref[0], gram_ref[1]
    eye = (iota((count, count), 0) == iota((count, count), 1)).astype(f32)
    zero = jnp.zeros((count, count), f32)
    work = jnp.concatenate([gram_r, gram_i, eye, zero], axis=1)
    turned = jnp.concatenate([-gram_i, gram_r, zero, eye], axis=1)
    row_ids = iota((count, 1), 0)
    roots = jnp.zeros((count, 1), f32)
    for pivot in range(count):
        lead = work[pivot:pivot + 1, pivot:pivot + 1]
        roots = jnp.where(row_ids == pivot, lead, roots)
        if pivot + 1 < count:
            below = jnp.where(row_ids > pivot, 1.0 / lead, 0.0)
            coef_r = work[:, pivot:pivot + 1] * below
            coef_i = work[:, count + pivot:count + pivot + 1] * below
            row, row_t = work[pivot:pivot + 1], turned[pivot:pivot + 1]
            work = work - (coef_r * row + coef_i * row_t)
            turned = turned - (coef_r * row_t - coef_i * row)
    back = work[:, 2 * count:] * (norm * lax.rsqrt(roots))
    back_r, back_i = back[:, :count], back[:, count:]
    full = jnp.concatenate([
        jnp.concatenate([back_r, -back_i], axis=1),
        jnp.concatenate([back_i, back_r], axis=1)], axis=0)
    full_top = full.astype(bf16)
    full_rest = (full - full_top.astype(f32)).astype(bf16)
    flat = sum_ref[...]
    flat_top = flat.astype(bf16)
    flat_rest = (flat - flat_top.astype(f32)).astype(bf16)
    left = jnp.concatenate([full_top, full_top, full_rest], axis=1)
    right = jnp.concatenate([flat_top, flat_rest, flat_top], axis=0)
    out_ref[...] = jnp.dot(left, right, preferred_element_type=f32)


def new_modes_of(gram, summed, norm):
    def kernel(gram_ref, sum_ref, out_ref):
        modes_kernel(norm, gram_ref, sum_ref, out_ref)

    return pl.pallas_call(
        kernel,
        out_shape=jax.ShapeDtypeStruct(summed.shape, f32),
        compiler_params=pltpu.CompilerParams(vmem_limit_bytes=8 << 20),
        cost_estimate=pl.CostEstimate(flops=1 << 27, bytes_accessed=1 << 20, transcendentals=256),
        name="orthonormal_modes",
    )(gram, summed)


def swap_tiles(value):
    count = lax.axis_size("tile")
    return lax.ppermute(value, "tile", [(i, (i + 1) % count) for i in range(count)])


def turn(value, step):
    count = lax.axis_size("scan")
    return lax.ppermute(value, "scan", [(i, (i + 2 * step) % count) for i in range(count)])


def across(value):
    count = lax.axis_size("scan")
    return lax.ppermute(value, "scan", [(i, i ^ 1) for i in range(count)])


def after(value, *others):
    return lax.optimization_barrier((value, *others))[0]


def gather_blocks(own, obj_b, cut, ready):
    come = {1: turn(own, 1), 3: turn(own, 3)}
    side = {0: across(own)}
    obj_pair = jnp.stack([obj_b, swap_tiles(obj_b)])
    patches = cut(obj_pair)
    patches, come[1], come[3], ready = lax.optimization_barrier((patches, come[1], come[3], ready))
    come[2] = turn(come[1], 1)
    for step in (3, 1, 2):
        side[step] = across(come[step])
    come[0] = own
    order = [-step % len(STEPS) for step in STEPS]
    mine = [come[step] for step in order] + [side[step] for step in order]
    return mine + [swap_tiles(value) for value in mine], patches, ready


def gather_any(own, obj_b, cut, ready):
    rows = own.shape[1]
    every = lax.all_gather(own, ("scan", "tile"))
    every = every.reshape((-1, RB // rows) + own.shape).transpose(0, 2, 1, 3, 4)
    every = every.reshape(-1, own.shape[0], RB, own.shape[2])
    blocks = [every[4 * step + 2 * y + tile] for tile in (0, 1) for y in (0, 1) for step in STEPS]
    return blocks, cut(jnp.stack([obj_b, swap_tiles(obj_b)])), ready


def gather_mixing(weights_b):
    wt_r, wt_i = jnp.swapaxes(weights_b[0], 0, 1), jnp.swapaxes(weights_b[1], 0, 1)
    real_rows = jnp.stack([wt_r, wt_i], axis=2)
    imag_rows = jnp.stack([-wt_i, wt_r], axis=2)
    count, cap = wt_r.shape
    return jnp.stack([real_rows, imag_rows], axis=0).reshape(2 * count, 2 * cap)


def scatter_sums(weights_b, updated, blocks):
    keep0, keep1, cross0, cross1 = updated
    pair = jnp.stack([weights_b, swap_tiles(weights_b)])
    pair = after(pair, blocks[-1])
    quad = jnp.concatenate([pair, across(pair)])
    wide = widen(jax.vmap(gather_mixing)(quad))
    order = (2, 3, 1, 0)
    at = {step: STEPS.index(step) for step in order}
    twin_cross = {step: swap_tiles(cross1[at[step]]) for step in order}
    twin = swap_tiles(keep1)
    far, far_twin, line = {}, {}, []
    for step in order:
        for value, dest in ((cross0[at[step]], far), (twin_cross[step], far_twin)):
            dest[step] = across(after(value, line[-DEPTH]) if len(line) >= DEPTH else value)
            line.append(dest[step])
    def part(step, kind):
        return pair_sums(at[step], wide, keep0, twin, far[step], far_twin[step], kind)

    through = turn(part(2, bf16), 1)
    third = turn(part(3, bf16), 3)
    first = turn((part(1, f32) + through.astype(f32)).astype(bf16), 1)
    return finish_sums(part(0, f32), [first, third])


def scatter_any(weights_b, updated, _):
    devices = lax.axis_size("scan") * lax.axis_size("tile")
    keep0, keep1, cross0, cross1 = updated
    count, slots, _, length = keep0.shape
    every = lax.all_gather(weights_b, ("scan", "tile"))
    rows = 4 * count * RB // devices
    parts = jnp.stack([keep0, keep1, jnp.stack(cross0), jnp.stack(cross1)], axis=1)
    parts = jnp.stack([parts[STEPS.index(step)] for step in range(count)])
    parts = parts.reshape(4 * count, slots, RB // rows, rows, length)
    parts = parts.transpose(0, 2, 1, 3, 4).reshape(devices, slots, rows, length)
    arrived = lax.all_to_all(parts, ("scan", "tile"), split_axis=0, concat_axis=0, tiled=True)
    flat = arrived.reshape(devices, slots // 2, 2, rows * length).astype(f32)
    wt_r, wt_i = every[:, 0].astype(f32), every[:, 1].astype(f32)
    up_r, up_i = flat[:, :, 0], flat[:, :, 1]

    def mul(left, right):
        return jnp.einsum("dpk,dpx->kx", left, right, precision=HI)

    sum_r = mul(wt_r, up_r) + mul(wt_i, up_i)
    sum_i = mul(wt_r, up_i) - mul(wt_i, up_r)

    def pair(left, right):
        return jnp.dot(left, right.T, precision=HI)

    gram = jnp.stack([pair(sum_r, sum_r) + pair(sum_i, sum_i),
                      pair(sum_i, sum_r) - pair(sum_r, sum_i)])
    return jnp.concatenate([sum_r, sum_i]), gram


def sum_everywhere(value, works):
    value = value + swap_tiles(value)
    count = lax.axis_size("scan")
    step, works = 1, list(works)
    results = []
    while step < count:
        come = lax.ppermute(value, "scan", [(i, i ^ step) for i in range(count)])
        step *= 2
        if works:
            value, come, result = lax.optimization_barrier((value, come, works.pop(0)(value)))
            results.append(result)
        value = value + come
    return value, results


def local(
    object_field, probe_modes, weights, amplitude, slot_count, tile_owner, corner_row, corner_col
):
    n_tile = lax.axis_size("tile")
    devices = lax.axis_size("scan") * n_tile
    tile = lax.axis_index("tile")
    cap, length, _ = amplitude.shape
    count = probe_modes.shape[1]
    pixels = length * length
    rows = length // devices
    forward, inverse = transform_tables(length)

    own = probe_modes.astype(bf16).reshape(2 * count, rows, length)
    obj_b = object_field.astype(bf16)
    weights_b = weights.astype(bf16)
    planned = lax.axis_size("scan") == 8 and n_tile == 2 and rows == RB

    scan = lax.axis_index("scan")
    zero = jnp.zeros_like(scan)
    meta = jnp.stack([tile, scan // 2, scan % 2, tile] if planned else [tile, zero, zero, zero])
    meta = meta.astype(jnp.int32)
    scalars = (meta, tile_owner, corner_row, corner_col)

    def cut(obj_pair):
        return cut_patches(obj_pair, scalars, cap, length)

    wt_r, wt_i = weights_b[0], weights_b[1]
    mix = jnp.stack([jnp.concatenate([wt_r, -wt_i], axis=1),
                     jnp.concatenate([wt_i, wt_r], axis=1)], axis=1)
    mix = widen(mix.reshape(1, 2 * cap, 2 * count))
    blocks, patches, (mix, forward, inverse) = (gather_blocks if planned else gather_any)(
        own, obj_b, cut, (mix, forward, inverse))
    updated, grads, stash = relax(meta, slot_count, mix, blocks, patches, amplitude, forward, inverse)

    def put_back(part):
        return lambda token: settle(scalars, after(grads[part], token), *object_field.shape[1:])

    summed, gram = (scatter_sums if planned else scatter_any)(weights_b, updated, blocks)

    def project(token):
        keep0, keep1, cross0, cross1 = updated
        return new_weights_of((after(keep0, token), keep1, cross0, cross1), stash)

    gram, (real, imag, new_weights) = sum_everywhere(gram, [put_back(0), put_back(1), project])
    steps = [mine_sum + swap_tiles(other_sum) for mine_sum, other_sum in (real, imag)]
    new_object = object_field + OBJ_STEP * jnp.stack(steps)
    new_modes = new_modes_of(gram, summed, math.sqrt(pixels)).reshape(probe_modes.shape)
    return (new_object, new_modes, new_weights)


def solution(mesh):
    in_specs = (
        P(None, ("groups", "scan", "tile"), None),
        P(None, "groups", ("scan", "tile")),
        P(None, ("groups", "scan", "tile"), None),
        P(("groups", "scan", "tile"), None, None),
        P(("groups", "scan")),
        P(("groups", "scan")),
        P(("groups", "scan")),
        P(("groups", "scan")),
    )
    out_specs = (
        P(None, ("groups", "scan", "tile"), None),
        P(None, "groups", ("scan", "tile")),
        P(None, ("groups", "scan", "tile"), None),
    )
    return jax.shard_map(local, mesh=mesh, in_specs=in_specs, out_specs=out_specs, check_vma=False)
```

```python
import math

import jax
import jax.numpy as jnp
import numpy as np
from jax import lax
from jax.experimental import pallas as pl
from jax.experimental.pallas import tpu as pltpu
from jax.sharding import PartitionSpec as P

OBJ_STEP = 0.125
PROBE_STEP = 0.5
RB = 16
DEPTH = 3
f32 = jnp.float32
bf16 = jnp.bfloat16
HI = lax.Precision.HIGHEST


def transform_tables(length):
    ids = np.arange(length)
    angles = (ids[:, None] * ids[None, :] % length) * (2.0 * math.pi / length)
    cos_tab = np.cos(angles) / math.sqrt(length)
    sin_tab = np.sin(angles) / math.sqrt(length)
    forward = np.block([[cos_tab, sin_tab], [-sin_tab, cos_tab]])
    inverse = np.block([[cos_tab, -sin_tab], [sin_tab, cos_tab]])
    return jnp.asarray(forward, dtype=bf16), jnp.asarray(inverse, dtype=bf16)


def iota(shape, dim):
    return lax.broadcasted_iota(jnp.int32, shape, dim)


def widen_kernel(tab_ref, out_ref):
    rows, cols = tab_ref.shape[1:]
    tall, wide = out_ref.shape[1:]
    up = (iota((tall, rows), 0) // RB == iota((tall, rows), 1)).astype(bf16)
    across = (iota((cols, wide), 1) // RB == iota((cols, wide), 0)).astype(bf16)
    same = iota((tall, wide), 0) % RB == iota((tall, wide), 1) % RB
    for at in range(tab_ref.shape[0]):
        left = jnp.dot(up, tab_ref[at], preferred_element_type=f32).astype(bf16)
        full = jnp.dot(left, across, preferred_element_type=f32)
        out_ref[at] = jnp.where(same, full, 0.0).astype(bf16)


def widen(tables):
    count, rows, cols = tables.shape
    return pl.pallas_call(
        widen_kernel,
        out_shape=jax.ShapeDtypeStruct((count, rows * RB, cols * RB), bf16),
        compiler_params=pltpu.CompilerParams(vmem_limit_bytes=8 << 20),
        cost_estimate=pl.CostEstimate(flops=1 << 28, bytes_accessed=1 << 20, transcendentals=0),
        name="widen",
    )(tables)


def cut_kernel(meta_ref, owner_ref, row_ref, col_ref, obj_ref, out_ref):
    spot = pl.program_id(0) + meta_ref[0] * pl.num_programs(0)
    length = out_ref.shape[2]
    height, width = obj_ref.shape[2:]
    row_at, col_at = row_ref[spot], col_ref[spot]
    sel = (owner_ref[spot] != meta_ref[0]).astype(jnp.int32)
    rows = (iota((length, height), 1) == iota((length, height), 0) + row_at).astype(bf16)
    cols = (iota((width, length), 0) == iota((width, length), 1) + col_at).astype(bf16)
    for part in range(2):
        band = jnp.dot(rows, obj_ref[sel, part], preferred_element_type=f32).astype(bf16)
        out_ref[0, part] = jnp.dot(band, cols, preferred_element_type=f32).astype(bf16)


def cut_patches(obj_pair, scalars, cap, length):
    grid_spec = pltpu.PrefetchScalarGridSpec(
        num_scalar_prefetch=4,
        grid=(cap,),
        in_specs=[pl.BlockSpec(obj_pair.shape, lambda i, *_: (0, 0, 0, 0))],
        out_specs=pl.BlockSpec((1, 2, length, length), lambda i, *_: (i, 0, 0, 0)),
    )
    return pl.pallas_call(
        cut_kernel,
        grid_spec=grid_spec,
        out_shape=jax.ShapeDtypeStruct((cap, 2, length, length), bf16),
        compiler_params=pltpu.CompilerParams(vmem_limit_bytes=12 << 20),
        cost_estimate=pl.CostEstimate(flops=4 << 30, bytes_accessed=4 << 20, transcendentals=0),
        name="cut_patches",
    )(*scalars, obj_pair)


STEPS = (0, 2, 3, 1)


def place_of(meta_ref, j):
    count = len(STEPS)
    side, far_side, place = j // (2 * count), j // count % 2, j % count
    z, y, first = meta_ref[1], meta_ref[2], meta_ref[3]
    strip = 2 * ((z + STEPS[place]) % count) + (1 - y if far_side else y)
    return 2 * strip + (1 - first if side else first)


def relax_kernel(meta_ref, live_ref, mix_ref, *refs):
    count = len(STEPS)
    tab = [place_of(meta_ref, j) for j in range(4 * count)]
    blocks, refs = refs[:4 * count], refs[4 * count:]
    patch_ref, amp_ref, fwd_ref, inv_ref, keep0_ref, keep1_ref = refs[:6]
    cross0, cross1 = refs[6:6 + count], refs[6 + count:6 + 2 * count]
    grad_r_ref, grad_i_ref, stash_ref, probe_ref, new_ref, stash_sem = refs[6 + 2 * count:]
    group = pl.program_id(0)
    each = patch_ref.shape[0]
    length = patch_ref.shape[2]

    @pl.when(group == 0)
    def _():
        mix = mix_ref[0]
        for j, block_ref in enumerate(blocks):
            block = block_ref[...].reshape(block_ref.shape[0] * RB, length)
            mixed = jnp.dot(mix, block, preferred_element_type=f32)
            at = pl.multiple_of(tab[j] * RB, RB)
            probe_ref[:, pl.ds(at, RB), :] = mixed.reshape(mixed.shape[0] // RB, RB, length)

    def stashing(j):
        return pltpu.make_async_copy(blocks[j], stash_ref.at[j], stash_sem.at[j])

    @pl.when(group == 0)
    def _():
        for j in range(len(blocks)):
            stashing(j).start()

    def planes(q):
        spot = each * group + q
        return (probe_ref[2 * spot], probe_ref[2 * spot + 1],
                patch_ref[q, 0].astype(f32), patch_ref[q, 1].astype(f32))

    def leave(q):
        probe_r, probe_i, obj_r, obj_i = planes(q)
        exit_r = (probe_r * obj_r - probe_i * obj_i).astype(bf16)
        exit_i = (probe_r * obj_i + probe_i * obj_r).astype(bf16)
        return exit_r, exit_i

    def rows_pass(table, pairs):
        both = jnp.concatenate([jnp.concatenate(pair, axis=0) for pair in pairs], axis=1)
        out = jnp.dot(table[...], both, preferred_element_type=f32).astype(bf16)
        return jnp.concatenate([
            jnp.concatenate([out[:length, q * length:(q + 1) * length],
                             out[length:, q * length:(q + 1) * length]], axis=1)
            for q in range(each)], axis=0)

    def cols_pass(table, value):
        out = jnp.dot(value, table[...], preferred_element_type=f32)
        return [out[q * length:(q + 1) * length] for q in range(each)]

    def revise(q, far):
        far_r, far_i = far[:, :length], far[:, length:]
        scale = amp_ref[q].astype(f32) * lax.rsqrt(far_r * far_r + far_i * far_i + 1.0)
        return (far_r * scale).astype(bf16), (far_i * scale).astype(bf16)

    def update(q, exits, near):
        live = (each * group + q < live_ref[meta_ref[0]]).astype(f32)
        probe_r, probe_i, obj_r, obj_i = planes(q)
        delta_r = near[:, :length] - exits[0].astype(f32)
        delta_i = near[:, length:] - exits[1].astype(f32)
        grad_r_ref[q] = ((probe_r * delta_r + probe_i * delta_i) * live).astype(bf16)
        grad_i_ref[q] = ((probe_r * delta_i - probe_i * delta_r) * live).astype(bf16)
        change_r = obj_r * delta_r + obj_i * delta_i
        change_i = obj_r * delta_i - obj_i * delta_r
        for part, value in ((0, probe_r + PROBE_STEP * change_r), (1, probe_i + PROBE_STEP * change_i)):
            new_ref[2 * q + part] = (value * live).astype(bf16).reshape(4 * count, RB, length)

    exits = [leave(q) for q in range(each)]
    far = cols_pass(inv_ref, rows_pass(fwd_ref, exits))
    revised = [revise(q, far[q]) for q in range(each)]
    near = cols_pass(fwd_ref, rows_pass(inv_ref, revised))
    for q in range(each):
        update(q, exits[q], near[q])
    @pl.when(group == pl.num_programs(0) - 1)
    def _():
        for j in range(len(blocks)):
            stashing(j).wait()

    for j in range(4 * count):
        at = tab[j]
        side, far_side, place = j // (2 * count), j // count % 2, j % count
        for row in range(2 * each):
            if far_side:
                (cross1 if side else cross0)[place][row] = new_ref[row, at]
            else:
                (keep1_ref if side else keep0_ref)[place, row] = new_ref[row, at]


def whole(arr):
    return pl.BlockSpec(arr.shape, lambda *_: (0,) * arr.ndim)


def relax(meta, live, mix, blocks, patches, amplitude, forward, inverse):
    cap, _, length, _ = patches.shape
    count = len(STEPS)
    each = 4 if cap % 4 == 0 else 1
    plane = pl.BlockSpec((each, 2, length, length), lambda i, *_: (i, 0, 0, 0))
    strips = pl.BlockSpec((count, 2 * each, RB, length), lambda i, *_: (0, i, 0, 0))
    strip = pl.BlockSpec((2 * each, RB, length), lambda i, *_: (i, 0, 0))
    flat = pl.BlockSpec((each, length, length), lambda i, *_: (i, 0, 0))
    grid_spec = pltpu.PrefetchScalarGridSpec(
        num_scalar_prefetch=2,
        grid=(cap // each,),
        in_specs=[
            whole(mix), *[whole(block) for block in blocks], plane,
            flat,
            whole(forward), whole(inverse),
        ],
        out_specs=[strips, strips, *[strip] * (2 * count), flat, flat,
                   pl.BlockSpec(memory_space=pl.ANY)],
        scratch_shapes=[
            pltpu.VMEM((2 * cap, length, length), f32),
            pltpu.VMEM((2 * each, 4 * count, RB, length), bf16),
            pltpu.SemaphoreType.DMA((len(blocks),)),
        ],
    )
    many = jax.ShapeDtypeStruct((count, 2 * cap, RB, length), bf16)
    single = jax.ShapeDtypeStruct((2 * cap, RB, length), bf16)
    outs = pl.pallas_call(
        relax_kernel,
        grid_spec=grid_spec,
        out_shape=[many, many, *[single] * (2 * count),
                   pltpu.HBM((cap, length, length), bf16),
                   pltpu.HBM((cap, length, length), bf16),
                   pltpu.HBM((len(blocks),) + blocks[0].shape, bf16)],
        compiler_params=pltpu.CompilerParams(vmem_limit_bytes=28 << 20),
        cost_estimate=pl.CostEstimate(flops=8 << 30, bytes_accessed=16 << 20, transcendentals=1 << 19),
        name="relax_positions",
    )(meta, live, mix, *blocks, patches, amplitude, forward, inverse)
    return (outs[0], outs[1], outs[2:2 + count], outs[2 + count:2 + 2 * count]), outs[-3:-1], outs[-1]


def settle_kernel(meta_ref, owner_ref, row_ref, col_ref, grad_ref, mine_ref, other_ref, band_ref):
    cap, length, _ = grad_ref.shape
    height, width = mine_ref.shape
    places = []
    for spot in range(cap):
        at = spot + meta_ref[0] * cap
        row_at, col_at = row_ref[at], col_ref[at]
        sel = (owner_ref[at] != meta_ref[0]).astype(jnp.int32)
        cols = (iota((length, width), 1) == iota((length, width), 0) + col_at).astype(bf16)
        band = jnp.dot(grad_ref[spot], cols, preferred_element_type=f32)
        band_ref[spot * length:(spot + 1) * length] = band.astype(bf16)
        place = iota((2 * height, length), 1) + row_at + height * sel
        places.append((iota((2 * height, length), 0) == place).astype(bf16))
    places = jnp.concatenate(places, axis=1)
    total = jnp.dot(places, band_ref[...], preferred_element_type=f32)
    mine_ref[...] = total[:height]
    other_ref[...] = total[height:]


def settle(scalars, grads, height, width):
    cap, length, _ = grads.shape
    tile = pl.BlockSpec((height, width), lambda *_: (0, 0))
    grid_spec = pltpu.PrefetchScalarGridSpec(
        num_scalar_prefetch=4,
        grid=(1,),
        in_specs=[whole(grads)],
        out_specs=[tile, tile],
        scratch_shapes=[pltpu.VMEM((cap * length, width), bf16)],
    )
    shape = jax.ShapeDtypeStruct((height, width), f32)
    return pl.pallas_call(
        settle_kernel,
        grid_spec=grid_spec,
        out_shape=[shape, shape],
        compiler_params=pltpu.CompilerParams(vmem_limit_bytes=20 << 20),
        cost_estimate=pl.CostEstimate(flops=2 << 30, bytes_accessed=4 << 20, transcendentals=0),
        name="settle",
    )(*scalars, grads)


def weights_kernel(keep0_ref, keep1_ref, *refs):
    count = len(STEPS)
    cross, (block_ref, nw_ref) = refs[:2 * count], refs[2 * count:]
    lanes = keep0_ref.shape[3]
    tall = keep0_ref.shape[1] * RB
    wide = block_ref.shape[1] * RB
    table = jnp.zeros((tall, wide), f32)
    for j in range(4 * count):
        side, far_side, place = j // (2 * count), j // count % 2, j % count
        if far_side:
            mine = cross[count * side + place][...]
        else:
            mine = (keep1_ref if side else keep0_ref)[place]
        table += lax.dot_general(mine.reshape(tall, lanes), block_ref[j].reshape(wide, lanes),
                                 (((1,), (1,)), ((), ())), preferred_element_type=f32)
    same = (iota((tall, wide), 0) % RB) == (iota((tall, wide), 1) % RB)
    table = jnp.where(same, table, 0.0)
    slots, modes = tall // (2 * RB), wide // (2 * RB)

    def mul(left, right):
        return jnp.dot(left, right, precision=HI, preferred_element_type=f32)

    def gather_rows(which):
        pick = iota((slots, tall), 1) // RB == 2 * iota((slots, tall), 0) + which
        return mul(pick.astype(f32), table)

    def pick_cols(which):
        pick = iota((wide, modes), 0) // RB == which * modes + iota((wide, modes), 1)
        return pick.astype(f32)

    low, high = gather_rows(0), gather_rows(1)
    cols_r, cols_i = pick_cols(0), pick_cols(1)
    norm = 1.0 / (4 * count * RB * lanes)
    nw_ref[0] = (mul(low, cols_r) + mul(high, cols_i)) * norm
    nw_ref[1] = (mul(high, cols_r) - mul(low, cols_i)) * norm


def new_weights_of(updated, blocks):
    keep0, keep1, cross0, cross1 = updated
    args = [keep0, keep1, *cross0, *cross1, blocks]
    return pl.pallas_call(
        weights_kernel,
        out_shape=jax.ShapeDtypeStruct((2, keep0.shape[1] // 2, blocks.shape[1] // 2), f32),
        compiler_params=pltpu.CompilerParams(vmem_limit_bytes=16 << 20),
        cost_estimate=pl.CostEstimate(flops=2 << 30, bytes_accessed=6 << 20, transcendentals=0),
        name="new_weights",
    )(*args)


def sums_kernel(wide_ref, near_ref, twin_ref, far_ref, far_twin_ref, out_ref):
    lanes = near_ref.shape[-1]

    def flat(value):
        return value.reshape(-1, lanes)

    total = jnp.dot(wide_ref[0], flat(near_ref[0]), preferred_element_type=f32)
    total += jnp.dot(wide_ref[1], flat(twin_ref[0]), preferred_element_type=f32)
    total += jnp.dot(wide_ref[2], flat(far_ref[...]), preferred_element_type=f32)
    total += jnp.dot(wide_ref[3], flat(far_twin_ref[...]), preferred_element_type=f32)
    out_ref[...] = total.reshape(out_ref.shape).astype(out_ref.dtype)


def pair_sums(place, wide, near, twin, far, far_twin, kind):
    lanes = near.shape[-1]
    strip = pl.BlockSpec((1,) + near.shape[1:], lambda i: (place, 0, 0, 0))
    tall = wide.shape[1] // RB
    return pl.pallas_call(
        sums_kernel,
        grid=(1,),
        in_specs=[whole(wide), strip, strip, whole(far), whole(far_twin)],
        out_specs=pl.BlockSpec((tall, RB, lanes), lambda *_: (0, 0, 0)),
        out_shape=jax.ShapeDtypeStruct((tall, RB, lanes), kind),
        compiler_params=pltpu.CompilerParams(vmem_limit_bytes=8 << 20),
        cost_estimate=pl.CostEstimate(flops=1 << 29, bytes_accessed=2 << 20, transcendentals=0),
        name="mode_sums",
    )(wide, near, twin, far, far_twin)


def finish_kernel(*refs):
    own_ref, others = refs[0], refs[1:-3]
    sum_ref, gram_ref, acc_ref = refs[-3:]
    lanes = own_ref.shape[-1]
    total = own_ref[...]
    for other in others:
        total = total + other[...].astype(f32)
    acc_ref[...] = total
    for row in range(RB):
        sum_ref[:, row * lanes:(row + 1) * lanes] = acc_ref[:, row, :]
    modes = sum_ref.shape[0] // 2
    flat = sum_ref[...]
    full = lax.dot_general(flat, flat, (((1,), (1,)), ((), ())), precision=HI,
                           preferred_element_type=f32)
    gram_ref[0] = full[:modes, :modes] + full[modes:, modes:]
    gram_ref[1] = full[modes:, :modes] - full[:modes, modes:]


def finish_sums(own, others):
    tall, _, lanes = own.shape
    return pl.pallas_call(
        finish_kernel,
        out_shape=[
            jax.ShapeDtypeStruct((tall, RB * lanes), f32),
            jax.ShapeDtypeStruct((2, tall // 2, tall // 2), f32),
        ],
        scratch_shapes=[pltpu.VMEM((tall, RB, lanes), f32)],
        compiler_params=pltpu.CompilerParams(vmem_limit_bytes=8 << 20),
        cost_estimate=pl.CostEstimate(flops=1 << 28, bytes_accessed=2 << 20, transcendentals=0),
        name="finish_sums",
    )(own, *others)


def modes_kernel(norm, gram_ref, sum_ref, out_ref):
    count = gram_ref.shape[1]
    gram_r, gram_i = gram_ref[0], gram_ref[1]
    eye = (iota((count, count), 0) == iota((count, count), 1)).astype(f32)
    zero = jnp.zeros((count, count), f32)
    work = jnp.concatenate([gram_r, gram_i, eye, zero], axis=1)
    turned = jnp.concatenate([-gram_i, gram_r, zero, eye], axis=1)
    row_ids = iota((count, 1), 0)
    roots = jnp.zeros((count, 1), f32)
    for pivot in range(count):
        lead = work[pivot:pivot + 1, pivot:pivot + 1]
        roots = jnp.where(row_ids == pivot, lead, roots)
        if pivot + 1 < count:
            below = jnp.where(row_ids > pivot, 1.0 / lead, 0.0)
            coef_r = work[:, pivot:pivot + 1] * below
            coef_i = work[:, count + pivot:count + pivot + 1] * below
            row, row_t = work[pivot:pivot + 1], turned[pivot:pivot + 1]
            work = work - (coef_r * row + coef_i * row_t)
            turned = turned - (coef_r * row_t - coef_i * row)
    back = work[:, 2 * count:] * (norm * lax.rsqrt(roots))
    back_r, back_i = back[:, :count], back[:, count:]
    full = jnp.concatenate([
        jnp.concatenate([back_r, -back_i], axis=1),
        jnp.concatenate([back_i, back_r], axis=1)], axis=0)
    full_top = full.astype(bf16)
    full_rest = (full - full_top.astype(f32)).astype(bf16)
    flat = sum_ref[...]
    flat_top = flat.astype(bf16)
    flat_rest = (flat - flat_top.astype(f32)).astype(bf16)
    left = jnp.concatenate([full_top, full_top, full_rest], axis=1)
    right = jnp.concatenate([flat_top, flat_rest, flat_top], axis=0)
    out_ref[...] = jnp.dot(left, right, preferred_element_type=f32)


def new_modes_of(gram, summed, norm):
    def kernel(gram_ref, sum_ref, out_ref):
        modes_kernel(norm, gram_ref, sum_ref, out_ref)

    return pl.pallas_call(
        kernel,
        out_shape=jax.ShapeDtypeStruct(summed.shape, f32),
        compiler_params=pltpu.CompilerParams(vmem_limit_bytes=8 << 20),
        cost_estimate=pl.CostEstimate(flops=1 << 27, bytes_accessed=1 << 20, transcendentals=256),
        name="orthonormal_modes",
    )(gram, summed)


def swap_tiles(value):
    count = lax.axis_size("tile")
    return lax.ppermute(value, "tile", [(i, (i + 1) % count) for i in range(count)])


def turn(value, step):
    count = lax.axis_size("scan")
    return lax.ppermute(value, "scan", [(i, (i + 2 * step) % count) for i in range(count)])


def across(value):
    count = lax.axis_size("scan")
    return lax.ppermute(value, "scan", [(i, i ^ 1) for i in range(count)])


def after(value, *others):
    return lax.optimization_barrier((value, *others))[0]


def gather_blocks(own, obj_b, cut, ready):
    come = {1: turn(own, 1), 3: turn(own, 3)}
    side = {0: across(own)}
    obj_pair = jnp.stack([obj_b, swap_tiles(obj_b)])
    patches = cut(obj_pair)
    patches, come[1], come[3], ready = lax.optimization_barrier((patches, come[1], come[3], ready))
    come[2] = turn(come[1], 1)
    for step in (1, 3, 2):
        side[step] = across(come[step])
    come[0] = own
    order = [-step % len(STEPS) for step in STEPS]
    mine = [come[step] for step in order] + [side[step] for step in order]
    return mine + [swap_tiles(value) for value in mine], patches, ready


def gather_any(own, obj_b, cut, ready):
    rows = own.shape[1]
    every = lax.all_gather(own, ("scan", "tile"))
    every = every.reshape((-1, RB // rows) + own.shape).transpose(0, 2, 1, 3, 4)
    every = every.reshape(-1, own.shape[0], RB, own.shape[2])
    blocks = [every[4 * step + 2 * y + tile] for tile in (0, 1) for y in (0, 1) for step in STEPS]
    return blocks, cut(jnp.stack([obj_b, swap_tiles(obj_b)])), ready


def gather_mixing(weights_b):
    wt_r, wt_i = jnp.swapaxes(weights_b[0], 0, 1), jnp.swapaxes(weights_b[1], 0, 1)
    real_rows = jnp.stack([wt_r, wt_i], axis=2)
    imag_rows = jnp.stack([-wt_i, wt_r], axis=2)
    count, cap = wt_r.shape
    return jnp.stack([real_rows, imag_rows], axis=0).reshape(2 * count, 2 * cap)


def scatter_sums(weights_b, updated, blocks):
    keep0, keep1, cross0, cross1 = updated
    pair = jnp.stack([weights_b, swap_tiles(weights_b)])
    pair = after(pair, blocks[-1])
    quad = jnp.concatenate([pair, across(pair)])
    wide = widen(jax.vmap(gather_mixing)(quad))
    order = (2, 3, 1, 0)
    at = {step: STEPS.index(step) for step in order}
    twin_cross = {step: swap_tiles(cross1[at[step]]) for step in order}
    twin = swap_tiles(keep1)
    far, far_twin, line = {}, {}, []
    for step in order:
        for value, dest in ((cross0[at[step]], far), (twin_cross[step], far_twin)):
            dest[step] = across(after(value, line[-DEPTH]) if len(line) >= DEPTH else value)
            line.append(dest[step])
    def part(step, kind):
        return pair_sums(at[step], wide, keep0, twin, far[step], far_twin[step], kind)

    through = turn(part(2, bf16), 1)
    third = turn(part(3, bf16), 3)
    first = turn((part(1, f32) + through.astype(f32)).astype(bf16), 1)
    return finish_sums(part(0, f32), [first, third])


def scatter_any(weights_b, updated, _):
    devices = lax.axis_size("scan") * lax.axis_size("tile")
    keep0, keep1, cross0, cross1 = updated
    count, slots, _, length = keep0.shape
    every = lax.all_gather(weights_b, ("scan", "tile"))
    rows = 4 * count * RB // devices
    parts = jnp.stack([keep0, keep1, jnp.stack(cross0), jnp.stack(cross1)], axis=1)
    parts = jnp.stack([parts[STEPS.index(step)] for step in range(count)])
    parts = parts.reshape(4 * count, slots, RB // rows, rows, length)
    parts = parts.transpose(0, 2, 1, 3, 4).reshape(devices, slots, rows, length)
    arrived = lax.all_to_all(parts, ("scan", "tile"), split_axis=0, concat_axis=0, tiled=True)
    flat = arrived.reshape(devices, slots // 2, 2, rows * length).astype(f32)
    wt_r, wt_i = every[:, 0].astype(f32), every[:, 1].astype(f32)
    up_r, up_i = flat[:, :, 0], flat[:, :, 1]

    def mul(left, right):
        return jnp.einsum("dpk,dpx->kx", left, right, precision=HI)

    sum_r = mul(wt_r, up_r) + mul(wt_i, up_i)
    sum_i = mul(wt_r, up_i) - mul(wt_i, up_r)

    def pair(left, right):
        return jnp.dot(left, right.T, precision=HI)

    gram = jnp.stack([pair(sum_r, sum_r) + pair(sum_i, sum_i),
                      pair(sum_i, sum_r) - pair(sum_r, sum_i)])
    return jnp.concatenate([sum_r, sum_i]), gram


def sum_everywhere(value, works):
    value = value + swap_tiles(value)
    count = lax.axis_size("scan")
    step, works = 1, list(works)
    results = []
    while step < count:
        come = lax.ppermute(value, "scan", [(i, i ^ step) for i in range(count)])
        step *= 2
        if works:
            value, come, result = lax.optimization_barrier((value, come, works.pop(0)(value)))
            results.append(result)
        value = value + come
    return value, results


def local(
    object_field, probe_modes, weights, amplitude, slot_count, tile_owner, corner_row, corner_col
):
    n_tile = lax.axis_size("tile")
    devices = lax.axis_size("scan") * n_tile
    tile = lax.axis_index("tile")
    cap, length, _ = amplitude.shape
    count = probe_modes.shape[1]
    pixels = length * length
    rows = length // devices
    forward, inverse = transform_tables(length)

    own = probe_modes.astype(bf16).reshape(2 * count, rows, length)
    obj_b = object_field.astype(bf16)
    weights_b = weights.astype(bf16)
    planned = lax.axis_size("scan") == 8 and n_tile == 2 and rows == RB

    scan = lax.axis_index("scan")
    zero = jnp.zeros_like(scan)
    meta = jnp.stack([tile, scan // 2, scan % 2, tile] if planned else [tile, zero, zero, zero])
    meta = meta.astype(jnp.int32)
    scalars = (meta, tile_owner, corner_row, corner_col)

    def cut(obj_pair):
        return cut_patches(obj_pair, scalars, cap, length)

    wt_r, wt_i = weights_b[0], weights_b[1]
    mix = jnp.stack([jnp.concatenate([wt_r, -wt_i], axis=1),
                     jnp.concatenate([wt_i, wt_r], axis=1)], axis=1)
    mix = widen(mix.reshape(1, 2 * cap, 2 * count))
    blocks, patches, (mix, forward, inverse) = (gather_blocks if planned else gather_any)(
        own, obj_b, cut, (mix, forward, inverse))
    updated, grads, stash = relax(meta, slot_count, mix, blocks, patches, amplitude, forward, inverse)

    def put_back(part):
        return lambda token: settle(scalars, after(grads[part], token), *object_field.shape[1:])

    summed, gram = (scatter_sums if planned else scatter_any)(weights_b, updated, blocks)

    def project(token):
        keep0, keep1, cross0, cross1 = updated
        return new_weights_of((after(keep0, token), keep1, cross0, cross1), stash)

    gram, (new_weights, real, imag) = sum_everywhere(gram, [project, put_back(0), put_back(1)])
    steps = [mine_sum + swap_tiles(other_sum) for mine_sum, other_sum in (real, imag)]
    new_object = object_field + OBJ_STEP * jnp.stack(steps)
    new_modes = new_modes_of(gram, summed, math.sqrt(pixels)).reshape(probe_modes.shape)
    return (new_object, new_modes, new_weights)


def solution(mesh):
    in_specs = (
        P(None, ("groups", "scan", "tile"), None),
        P(None, "groups", ("scan", "tile")),
        P(None, ("groups", "scan", "tile"), None),
        P(("groups", "scan", "tile"), None, None),
        P(("groups", "scan")),
        P(("groups", "scan")),
        P(("groups", "scan")),
        P(("groups", "scan")),
    )
    out_specs = (
        P(None, ("groups", "scan", "tile"), None),
        P(None, "groups", ("scan", "tile")),
        P(None, ("groups", "scan", "tile"), None),
    )
    return jax.shard_map(local, mesh=mesh, in_specs=in_specs, out_specs=out_specs, check_vma=False)
```
